32 devices in a mesh: obs: 8 (over z, x), sub: 4 (over y, core).
Axes of the slice: x: 2, y: 2, z: 4, core: 2. Of those that a mesh axis runs over, the one named last changes fastest.
Arguments:
- jacobian: bfloat16 [32768, 2048], P(('obs', 'sub')), may hold values from -0.09375 to 0.09375
- obs_weight: float32 [32768], P(('obs', 'sub')), may hold values from 0.2 to 5
- row_counts: int32 [8], P('obs'), may hold values from 1 to 4096, 24576 in all
- tile_lists: int32 [8, 8], replicated, may hold values from 0 to 15, all different within a row
- tile_slot: int32 [16], replicated, may hold values from 0 to 15, each once
- probe_block: bfloat16 [4096, 256], P('obs'), may hold values from -6 to 6
Outputs:
- owned_product: bfloat16 [4096, 256], P('obs', 'sub')
The draws below stay inside these ranges and needn't reach their ends.
Inputs may be any that keep to these rules, and one draw needn't show every extreme that they name: `row_counts`: the live counts of one block; some block is full (4096) in every draw. `tile_lists`: each row lists 8 different tiles; every tile is listed by some block. `tile_slot`: a permutation of the tiles.
All inputs are finite; a program needn't handle non-finite values.
Results may differ from the reference program's by a relative error of at most 0.0034.
Values may be sent and summed in bfloat16 or wider, within the bound.
No kernel may reach another device: no remote copies, remote signals or barrier semaphores. Data moves between devices by JAX's collectives and lax.ppermute only.
A program may use at most 64 MiB of HBM per device.

```python
import math
import jax
import jax.numpy as jnp
import numpy as np
from jax import lax

TILE = 256
PROBE = 256
KT = 8
NT = 16
ROWS = 1024
BLOCK = 4096
KC = 2048
OBS_ALL = 32768
N_OBS = 8


def level_of(stream_key, shape, split, least, top_value):
    def one(axis_at, parts):
        steps = jax.random.uniform(jax.random.fold_in(jax.random.fold_in(stream_key, 6), axis_at), (parts,), jnp.float32, least / len(split), top_value / len(split))
        return jnp.repeat(jnp.exp(steps), shape[axis_at] // parts).reshape((-1,) + (1,) * (len(shape) - axis_at - 1))

    loudness = one(*split[0])
    for cut in split[1:]:
        loudness = loudness * one(*cut)
    return loudness


def choose_distinct(key, rows, count, top, lift):
    order = jax.random.permutation(jax.random.fold_in(key, 1), count)
    favour = order
    for power in range(3):
        favour = favour * favour // count
    favour = favour * lift // count
    chance = jax.random.randint(jax.random.fold_in(key, 2), (rows, count), 0, 4096) + favour
    sure = jax.random.permutation(jax.random.fold_in(key, 3), rows)[jnp.arange(count) % rows]
    chance = jnp.where(jnp.arange(rows)[:, None] == sure[None, :], 1 << 14, chance)
    score = chance * count + jnp.arange(count)
    return lax.top_k(score.astype(jnp.int32), top)[1].astype(jnp.int32)


def length_profile(count, total, bound, slope):
    weights = [(1 << 20) // math.isqrt(grade ** slope) + 1 for grade in range(2, count + 1)]
    spare, given = total - bound - (count - 1), [1] * (count - 1)
    while spare > 0:
        candidates = [i for i in range(count - 1) if given[i] < bound]
        pool, budget = sum([weights[i] for i in candidates]), spare
        for i in candidates:
            extra = min(bound - given[i], max(1, budget * weights[i] // pool), spare)
            given[i] = given[i] + extra
            spare = spare - extra
    return np.array([bound] + given)


def ragged_sizes(stream_key, number_of, total, limit, lean):
    if number_of == 2:
        one = jax.random.randint(stream_key, (), max(1, total - limit), min(limit, total - 1) + 1)
        return jnp.stack([one, total - one])
    lengths = jnp.asarray(length_profile(number_of, total, limit, lean), jnp.int32)
    twos = (number_of - 1) // 2
    source_of, receiver = lengths[1:1 + 2 * twos:2], lengths[2:2 + 2 * twos:2]
    slack = jnp.minimum(source_of - 1, limit - receiver)
    shifted = jax.random.randint(jax.random.fold_in(stream_key, 1), (twos,), 0, 1 << 20) % (slack + 1)
    lengths = lengths.at[1:1 + 2 * twos:2].set(source_of - shifted).at[2:2 + 2 * twos:2].set(receiver + shifted)
    return lengths[jax.random.permutation(jax.random.fold_in(stream_key, 2), number_of)]


def normal_values(own_key, dims, spread, reach, split=(), held_as=jnp.bfloat16):
    loudness = level_of(own_key, dims, split, -0.22, 0.18) if split else 1.0
    values = jax.random.normal(own_key, dims, jnp.float32) * spread * loudness
    return jnp.minimum(jnp.maximum(values, -reach), reach).astype(held_as)


def setup_inputs(seed: int = 0) -> dict:
    streams_of = jax.random.split(jax.random.key(seed), 7)
    return {
        "jacobian": normal_values(streams_of[0], (OBS_ALL, KC), BLOCK ** -0.5, 0.09375, ((0, 32),)),
        "obs_weight": jnp.clip(jnp.exp(math.log(5.0) - 3.218876 * jax.random.uniform(streams_of[1], (OBS_ALL,), jnp.float32) ** level_of(streams_of[1], (OBS_ALL,), ((0, 32),), -0.2, 0.2)), 0.2, 5.0),
        "row_counts": ragged_sizes(streams_of[2], N_OBS, 3 * N_OBS * ROWS, BLOCK, 2).astype(jnp.int32),
        "tile_lists": choose_distinct(streams_of[3], N_OBS, NT, KT, 8192),
        "tile_slot": jax.random.permutation(streams_of[4], NT).astype(jnp.int32),
        "probe_block": normal_values(streams_of[5], (NT * TILE, PROBE), 1.0, 6.0, ((0, 8),)),
    }


def reference(jacobian, obs_weight, row_counts, tile_lists, tile_slot, probe_block):
    blocks = jacobian.reshape(N_OBS, BLOCK, KC)
    weights = obs_weight.reshape(N_OBS, BLOCK)
    probe_tiles = probe_block.reshape(NT, TILE, PROBE)

    def one_block(inputs):
        jac_block, weight_block, count, columns = inputs
        live = (jnp.arange(BLOCK, dtype=jnp.int32) < count).astype(jnp.float32)
        weighted = (jac_block.astype(jnp.float32) * (weight_block * live)[:, None]).astype(jnp.bfloat16)
        probe_cols = probe_tiles[columns.astype(jnp.int32)].reshape(KC, PROBE)
        image = jnp.dot(jac_block, probe_cols, preferred_element_type=jnp.float32).astype(jnp.bfloat16)
        contrib = lax.dot_general(weighted, image, (((0,), (0,)), ((), ())),
                                  preferred_element_type=jnp.float32)
        return contrib.reshape(KT, TILE, PROBE)

    contribs = lax.map(one_block, (blocks, weights, row_counts, tile_lists))
    product = jnp.zeros((NT, TILE, PROBE), jnp.float32)
    product = product.at[tile_lists.reshape(-1).astype(jnp.int32)].add(
        contribs.reshape(N_OBS * KT, TILE, PROBE).astype(jnp.float32))
    placed = jnp.zeros((NT, TILE, PROBE), jnp.float32).at[tile_slot.astype(jnp.int32)].set(product)
    return placed.reshape(NT * TILE, PROBE).astype(jnp.bfloat16)
```

```python
import functools

import jax
import jax.numpy as jnp
from jax import lax
from jax.experimental import pallas as pl
from jax.experimental.pallas import tpu as pltpu
from jax.sharding import PartitionSpec as P

VMEM_LIMIT = 40 * 1024 * 1024


def swap(value, axis, count, step):
    return lax.ppermute(value, axis, [(i, i ^ step) for i in range(count)])


def pick_kernel(unit, tile, subs, obs_count, ids, lists, *refs):
    pieces, out, position = refs[:obs_count], refs[obs_count], refs[obs_count + 1]
    block = ids[0]
    listed = lists.shape[1]
    part = unit // subs
    units = pieces[0].shape[0] // part
    for a in range(position.shape[0]):
        position[a] = -1
    for k in range(listed):
        position[lists[block, k]] = k
    for step in range(obs_count):
        owner = block ^ step
        for u in range(units):
            row = (owner * units + u) * unit
            at = position[row // tile]
            inside = (row % tile) // subs

            @pl.when(at >= 0)
            def _():
                first = pl.multiple_of(at * (tile // subs) + inside, part)
                out[pl.ds(first, part), :] = pieces[step][u * part:(u + 1) * part, :]


def product_kernel(unit, tile, subs, ids, weight, jac, *refs):
    pieces, outs = refs[:subs], refs[subs:2 * subs]
    probe, image_t, weighted, product, held, sems = refs[2 * subs:]
    sub, count = ids[1], ids[2]
    rows, width = held.shape
    chunk = rows // sems.shape[0]
    copies = [
        pltpu.make_async_copy(jac.at[pl.ds(i * chunk, chunk)], held.at[pl.ds(i * chunk, chunk)], sems.at[i])
        for i in range(sems.shape[0])
    ]
    for copy in copies:
        copy.start()
    part = unit // subs
    for j in range(subs):
        other = sub ^ j
        for g in range(width // unit):
            first = pl.multiple_of(g * unit + other * part, part)
            probe[pl.ds(first, part), :] = pieces[j][g * part:(g + 1) * part, :]
    lanes = weight.shape[1]
    for i, copy in enumerate(copies):
        copy.wait()
        for r in range(i * chunk, (i + 1) * chunk, lanes):
            at = sub * rows + r + lax.broadcasted_iota(jnp.int32, (lanes, lanes), 0)
            scale = jnp.broadcast_to(weight[r // lanes:r // lanes + 1, :], (lanes, lanes)).T
            scale = scale * (at < count).astype(jnp.float32)
            scale = jnp.concatenate([scale] * (width // lanes), axis=1)
            weighted[r:r + lanes, :] = (held[r:r + lanes, :].astype(jnp.float32) * scale).astype(jnp.bfloat16)
        image = jnp.dot(held[i * chunk:(i + 1) * chunk, :], probe[...], preferred_element_type=jnp.float32)
        image_t[:, i * chunk:(i + 1) * chunk] = image.astype(jnp.bfloat16).T
    columns = 2 * tile

    @pl.loop(0, width // columns)
    def _(n):
        span = pl.ds(pl.multiple_of(n * columns, columns), columns)
        product[:, span] = jnp.dot(image_t[...], weighted[:, span], preferred_element_type=jnp.float32)

    high = product.shape[0] // subs
    for j in range(subs):
        first = pl.multiple_of((sub ^ j) * high, high)
        outs[j][...] = product[pl.ds(first, high), :].astype(outs[j].dtype)


def place_kernel(unit, tile, ids, lists, slots, *refs):
    parts, out, position, total = refs[:-3], refs[-3], refs[-2], refs[-1]
    block = ids[0]
    for a in range(position.shape[0]):
        position[a] = -1
    for k in range(lists.shape[1]):
        position[slots[lists[block, k]]] = k
    value = parts[0][...].astype(jnp.float32)
    for part in parts[1:]:
        value = value + part[...].astype(jnp.float32)
    total[...] = value
    units = out.shape[2] // unit
    for owner in range(out.shape[0]):
        for u in range(units):
            row = (owner * units + u) * unit
            at = position[row // tile]
            first = pl.multiple_of(jnp.maximum(at, 0) * tile, tile)
            taken = total[:, pl.ds(first, tile)]
            taken = jnp.where(at >= 0, taken, 0.0).astype(out.dtype)
            out[owner, :, u * unit:(u + 1) * unit] = taken[:, row % tile:row % tile + unit]


def local(obs_count, subs, jacobian, obs_weight, row_counts, tile_lists, tile_slot, probe_block):
    rows, width = jacobian.shape
    tiles = tile_slot.shape[0]
    tile = width // tile_lists.shape[1]
    own_rows, probe_width = probe_block.shape
    unit = min(own_rows, tile)
    part = unit // subs
    block, sub = lax.axis_index("obs"), lax.axis_index("sub")
    ids = jnp.stack([block, sub, row_counts[0]])
    smem, vmem = pl.BlockSpec(memory_space=pltpu.SMEM), pl.BlockSpec(memory_space=pltpu.VMEM)
    params = pltpu.CompilerParams(vmem_limit_bytes=VMEM_LIMIT)

    mine = probe_block.reshape(own_rows // unit, subs, part, probe_width)
    mine = lax.dynamic_index_in_dim(mine, sub, 1, keepdims=False).reshape(own_rows // subs, probe_width)
    pieces = [mine] + [swap(mine, "obs", obs_count, step) for step in range(1, obs_count)]
    picked = pl.pallas_call(
        functools.partial(pick_kernel, unit, tile, subs, obs_count),
        out_shape=jax.ShapeDtypeStruct((width // subs, probe_width), jnp.bfloat16),
        in_specs=[smem, smem] + [vmem] * obs_count,
        out_specs=vmem,
        scratch_shapes=[pltpu.SMEM((tiles,), jnp.int32)],
        compiler_params=params,
        name="pick_listed",
    )(ids, tile_lists, *pieces)

    columns = {0: picked}
    step = subs // 2
    while step:
        have = sorted(columns)
        got = swap(jnp.stack([columns[j] for j in have]), "sub", subs, step)
        for i, j in enumerate(have):
            columns[j ^ step] = got[i]
        step //= 2

    lanes = min(128, rows)
    high = probe_width // subs
    partial = pl.pallas_call(
        functools.partial(product_kernel, unit, tile, subs),
        out_shape=[jax.ShapeDtypeStruct((high, width), jnp.float32 if j == 0 else jnp.bfloat16) for j in range(subs)],
        in_specs=[smem, vmem, pl.BlockSpec(memory_space=pl.ANY)] + [vmem] * subs,
        out_specs=[vmem] * subs,
        scratch_shapes=[
            pltpu.VMEM((width, probe_width), jnp.bfloat16),
            pltpu.VMEM((probe_width, rows), jnp.bfloat16),
            pltpu.VMEM((rows, width), jnp.bfloat16),
            pltpu.VMEM((probe_width, width), jnp.float32),
            pltpu.VMEM((rows, width), jnp.bfloat16),
            pltpu.SemaphoreType.DMA((4,)),
        ],
        compiler_params=params,
        name="product",
    )(ids, obs_weight.reshape(rows // lanes, lanes), jacobian, *[columns[j] for j in range(subs)])

    arrived = [partial[0]] + [swap(partial[j], "sub", subs, j) for j in range(1, subs)]
    placed = pl.pallas_call(
        functools.partial(place_kernel, unit, tile),
        out_shape=jax.ShapeDtypeStruct((obs_count, high, own_rows), jnp.bfloat16),
        in_specs=[smem] * 3 + [vmem] * subs,
        out_specs=vmem,
        scratch_shapes=[pltpu.SMEM((tiles,), jnp.int32), pltpu.VMEM((high, width), jnp.float32)],
        compiler_params=params,
        name="place",
    )(ids, tile_lists, tile_slot, *arrived)
    shares = lax.all_to_all(placed, "obs", 0, 0, tiled=True)
    summed = jnp.sum(shares.astype(jnp.float32), axis=0)
    return summed.T.astype(jnp.bfloat16)


def solution(mesh):
    placed = (P(("obs", "sub"), None), P(("obs", "sub")), P("obs"), P(), P(), P("obs", None))
    return jax.shard_map(
        functools.partial(local, mesh.shape["obs"], mesh.shape["sub"]),
        mesh=mesh, in_specs=placed, out_specs=P("obs", "sub"), check_vma=False,
    )
```

```python
import functools

import jax
import jax.numpy as jnp
from jax import lax
from jax.experimental import pallas as pl
from jax.experimental.pallas import tpu as pltpu
from jax.sharding import PartitionSpec as P

CHUNKS = 2
MIB = 1024 * 1024
SMEM = pl.BlockSpec(memory_space=pltpu.SMEM)
VMEM = pl.BlockSpec(memory_space=pltpu.VMEM)
HBM = pl.BlockSpec(memory_space=pltpu.HBM)


def swap(value, axis, count, step):
    return lax.ppermute(value, axis, [(i, i ^ step) for i in range(count)])


def far_steps(count):
    return [2 * high for high in range(count // 2 - 1, 0, -1)]


def spread(value, axis, count):
    held = {0: value}
    for step in far_steps(count):
        held[step] = swap(value, axis, count, step)
    held[1] = swap(value, axis, count, 1)
    for step in far_steps(count):
        held[step + 1] = swap(held[step], axis, count, 1)
    return [held[step] for step in range(count)]


def collect(terms, axis, count):
    parts = [terms[0]]
    for step in far_steps(count):
        passed = swap(terms[step + 1], axis, count, 1)
        both = (terms[step] + passed.astype(jnp.float32)).astype(jnp.bfloat16)
        parts.append(swap(both, axis, count, step))
    parts.append(swap(terms[1], axis, count, 1))
    return parts


def split_kernel(unit, subs, probe, *refs):
    outs, rows, sems = refs[:-2], refs[-2], refs[-1]
    sub = lax.axis_index("sub")
    part = unit // subs
    copies = [
        pltpu.make_async_copy(
            probe.at[pl.ds(pl.multiple_of(u * unit + sub * part, part), part)],
            rows.at[pl.ds(u * part, part)], sems.at[u])
        for u in range(sems.shape[0])
    ]
    for copy in copies:
        copy.start()
    width = rows.shape[1]
    lanes = width // len(outs)
    high, low = width // subs, lanes // subs
    source = lax.broadcasted_iota(jnp.int32, (width, lanes), 0)
    target = lax.broadcasted_iota(jnp.int32, (width, lanes), 1)
    wanted = (target // low) * high + target % low
    chosen = [(source == wanted + c * low).astype(jnp.bfloat16) for c in range(len(outs))]
    for copy in copies:
        copy.wait()
    for c, out in enumerate(outs):
        out[...] = jnp.dot(rows[...], chosen[c], preferred_element_type=jnp.float32).astype(out.dtype)


def weigh_kernel(count, weight, jac, held, weighted, sems):
    rows, width = held.shape
    chunk = rows // sems.shape[0]
    copies = [
        pltpu.make_async_copy(jac.at[pl.ds(i * chunk, chunk)], held.at[pl.ds(i * chunk, chunk)], sems.at[i])
        for i in range(sems.shape[0])
    ]
    for copy in copies:
        copy.start()
    sub = lax.axis_index("sub")
    lanes = weight.shape[1]
    for i, copy in enumerate(copies):
        copy.wait()
        for r in range(i * chunk, (i + 1) * chunk, lanes):
            at = sub * rows + r + lax.broadcasted_iota(jnp.int32, (lanes, lanes), 0)
            scale = jnp.broadcast_to(weight[r // lanes:r // lanes + 1, :], (lanes, lanes)).T
            scale = scale * (at < count[0]).astype(jnp.float32)
            scale = jnp.concatenate([scale] * (width // lanes), axis=1)
            weighted[r:r + lanes, :] = (held[r:r + lanes, :].astype(jnp.float32) * scale).astype(jnp.bfloat16)


def pick_kernel(unit, tile, subs, listed, info, *refs):
    pieces, out, position = refs[:-2], refs[-2], refs[-1]
    block = lax.axis_index("obs")
    part = unit // subs
    units = pieces[0].shape[0] // part
    for a in range(position.shape[0]):
        position[a] = -1
    for k in range(listed):
        position[info[k]] = k
    for step, piece in enumerate(pieces):
        for u in range(units):
            row = ((block ^ step) * units + u) * unit
            at = position[row // tile]

            @pl.when(at >= 0)
            def _():
                first = pl.multiple_of(at * (tile // subs) + (row % tile) // subs, part)
                out[pl.ds(first, part), :] = piece[u * part:(u + 1) * part, :]


def product_kernel(unit, subs, held, weighted, *refs):
    pieces, outs = refs[:subs], refs[subs:2 * subs]
    probe, product = refs[2 * subs:]
    sub = lax.axis_index("sub")
    width = held.shape[1]
    part = unit // subs
    for j in range(subs):
        for g in range(width // unit):
            first = pl.multiple_of(g * unit + (sub ^ j) * part, part)
            probe[pl.ds(first, part), :] = pieces[j][g * part:(g + 1) * part, :]
    image = jnp.dot(held[...], probe[...], preferred_element_type=jnp.float32)
    image_t = image.astype(jnp.bfloat16).T
    product[...] = jnp.dot(image_t, weighted[...], preferred_element_type=jnp.float32)
    high = product.shape[0] // subs
    for j in range(subs):
        first = pl.multiple_of((sub ^ j) * high, high)
        outs[j][...] = product[pl.ds(first, high), :].astype(outs[j].dtype)


def place_kernel(unit, tile, listed, parts_count, info, *refs):
    parts, outs = refs[:parts_count], refs[parts_count:-2]
    position, total = refs[-2:]
    block = lax.axis_index("obs")
    for a in range(position.shape[0]):
        position[a] = -1
    for k in range(listed):
        position[info[listed + info[k]]] = k
    value = parts[0][...]
    for term in parts[1:]:
        value = value + term[...].astype(jnp.float32)
    total[...] = value
    units = outs[0].shape[1] // unit
    for step, out in enumerate(outs):
        for u in range(units):
            row = ((block ^ step) * units + u) * unit
            at = position[row // tile]
            first = pl.multiple_of(jnp.maximum(at, 0) * tile, tile)
            whole = jnp.where(at >= 0, total[:, pl.ds(first, tile)], 0.0)
            taken = whole[:, :unit]
            for q in range(1, tile // unit):
                taken = jnp.where(row % tile == q * unit, whole[:, q * unit:(q + 1) * unit], taken)
            out[:, u * unit:(u + 1) * unit] = taken.astype(out.dtype)


def kept(step):
    return jnp.float32 if step % 2 == 0 else jnp.bfloat16


def local(obs_count, subs, jacobian, obs_weight, row_counts, tile_lists, tile_slot, probe_block):
    rows, width = jacobian.shape
    tiles = tile_slot.shape[0]
    listed = tile_lists.shape[1]
    tile = width // listed
    own_rows, probe_width = probe_block.shape
    unit = min(own_rows, tile)
    lanes = probe_width // CHUNKS
    high = lanes // subs
    my_list = lax.dynamic_index_in_dim(tile_lists, lax.axis_index("obs"), 0, keepdims=False)
    info = jnp.concatenate([my_list, tile_slot])

    def params(mib):
        return pltpu.CompilerParams(vmem_limit_bytes=mib * MIB)

    shares = pl.pallas_call(
        functools.partial(split_kernel, unit, subs),
        out_shape=[jax.ShapeDtypeStruct((own_rows // subs, lanes), jnp.bfloat16)] * CHUNKS,
        in_specs=[HBM],
        out_specs=[VMEM] * CHUNKS,
        scratch_shapes=[
            pltpu.VMEM((own_rows // subs, probe_width), jnp.bfloat16),
            pltpu.SemaphoreType.DMA((own_rows // unit,)),
        ],
        compiler_params=params(8),
        name="split_probe",
    )(probe_block)
    weight_lanes = min(128, rows)
    held, weighted = pl.pallas_call(
        weigh_kernel,
        out_shape=[jax.ShapeDtypeStruct((rows, width), jnp.bfloat16)] * 2,
        in_specs=[SMEM, VMEM, HBM],
        out_specs=[VMEM, VMEM],
        scratch_shapes=[pltpu.SemaphoreType.DMA((4,))],
        compiler_params=params(16),
        cost_estimate=pl.CostEstimate(flops=2 * rows * width, bytes_accessed=6 * rows * width, transcendentals=0),
        name="weigh",
    )(row_counts, obs_weight.reshape(rows // weight_lanes, weight_lanes), jacobian)

    pick = pl.pallas_call(
        functools.partial(pick_kernel, unit, tile, subs, listed),
        out_shape=jax.ShapeDtypeStruct((width // subs, lanes), jnp.bfloat16),
        in_specs=[SMEM] + [VMEM] * obs_count,
        out_specs=VMEM,
        scratch_shapes=[pltpu.SMEM((tiles,), jnp.int32)],
        compiler_params=params(8),
        name="pick_listed",
    )
    product = pl.pallas_call(
        functools.partial(product_kernel, unit, subs),
        out_shape=[jax.ShapeDtypeStruct((high, width), kept(j)) for j in range(subs)],
        in_specs=[VMEM] * (2 + subs),
        out_specs=[VMEM] * subs,
        scratch_shapes=[
            pltpu.VMEM((width, lanes), jnp.bfloat16),
            pltpu.VMEM((lanes, width), jnp.float32),
        ],
        compiler_params=params(24),
        cost_estimate=pl.CostEstimate(
            flops=4 * rows * width * lanes, bytes_accessed=4 * rows * width, transcendentals=0),
        name="product",
    )
    place = pl.pallas_call(
        functools.partial(place_kernel, unit, tile, listed, subs // 2 + 1),
        out_shape=[jax.ShapeDtypeStruct((high, own_rows), kept(step)) for step in range(obs_count)],
        in_specs=[SMEM] + [VMEM] * (subs // 2 + 1),
        out_specs=[VMEM] * obs_count,
        scratch_shapes=[pltpu.SMEM((tiles,), jnp.int32), pltpu.VMEM((high, width), jnp.float32)],
        compiler_params=params(8),
        name="place",
    )

    pieces = [spread(share, "obs", obs_count) for share in shares]
    columns = [spread(pick(info, *piece), "sub", subs) for piece in pieces]
    partial = [product(held, weighted, *column) for column in columns]
    blocks = [collect(terms, "sub", subs) for terms in partial]
    placed = [collect(place(info, *terms), "obs", obs_count) for terms in blocks]
    sums = [sum(term.astype(jnp.float32) for term in terms).astype(jnp.bfloat16) for terms in placed]
    return jnp.concatenate(sums, axis=0).T


def solution(mesh):
    placed = (P(("obs", "sub"), None), P(("obs", "sub")), P("obs"), P(), P(), P("obs", None))
    return jax.shard_map(
        functools.partial(local, mesh.shape["obs"], mesh.shape["sub"]),
        mesh=mesh, in_specs=placed, out_specs=P("obs", "sub"), check_vma=False,
    )
```

```python
import functools

import jax
import jax.numpy as jnp
from jax import lax
from jax.experimental import pallas as pl
from jax.experimental.pallas import tpu as pltpu
from jax.sharding import PartitionSpec as P

MIB = 1024 * 1024
SMEM = pl.BlockSpec(memory_space=pltpu.SMEM)
VMEM = pl.BlockSpec(memory_space=pltpu.VMEM)
HBM = pl.BlockSpec(memory_space=pltpu.HBM)


def swap(value, axis, count, step):
    return lax.ppermute(value, axis, [(i, i ^ step) for i in range(count)])


def far_steps(count):
    return [2 * high for high in range(count // 2 - 1, 0, -1)]


def spread(value, axis, count):
    held = {0: value}
    for step in far_steps(count):
        held[step] = swap(value, axis, count, step)
    held[1] = swap(value, axis, count, 1)
    for step in far_steps(count):
        held[step + 1] = swap(held[step], axis, count, 1)
    return [held[step] for step in range(count)]


def collect(terms, axis, count):
    parts = [terms[0]]
    for step in far_steps(count):
        passed = swap(terms[step + 1], axis, count, 1)
        both = (terms[step] + passed.astype(jnp.float32)).astype(jnp.bfloat16)
        parts.append(swap(both, axis, count, step))
    parts.append(swap(terms[1], axis, count, 1))
    return parts


def share_kernel(unit, subs, probe, out, sems):
    sub = lax.axis_index("sub")
    part = unit // subs
    copies = [
        pltpu.make_async_copy(
            probe.at[pl.ds(pl.multiple_of(u * unit + sub * part, part), part)],
            out.at[pl.ds(u * part, part)], sems.at[u])
        for u in range(sems.shape[0])
    ]
    for copy in copies:
        copy.start()
    for copy in copies:
        copy.wait()


def weigh_kernel(count, weight, jac, held, weighted, sems):
    rows, width = held.shape
    chunk = rows // sems.shape[0]
    copies = [
        pltpu.make_async_copy(jac.at[pl.ds(i * chunk, chunk)], held.at[pl.ds(i * chunk, chunk)], sems.at[i])
        for i in range(sems.shape[0])
    ]
    for copy in copies:
        copy.start()
    sub = lax.axis_index("sub")
    lanes = weight.shape[1]
    for i, copy in enumerate(copies):
        copy.wait()
        for r in range(i * chunk, (i + 1) * chunk, lanes):
            at = sub * rows + r + lax.broadcasted_iota(jnp.int32, (lanes, lanes), 0)
            scale = jnp.broadcast_to(weight[r // lanes:r // lanes + 1, :], (lanes, lanes)).T
            scale = scale * (at < count[0]).astype(jnp.float32)
            scale = jnp.concatenate([scale] * (width // lanes), axis=1)
            weighted[r:r + lanes, :] = (held[r:r + lanes, :].astype(jnp.float32) * scale).astype(jnp.bfloat16)


def pick_kernel(unit, tile, subs, listed, info, ready, *refs):
    pieces, out, position = refs[:-2], refs[-2], refs[-1]
    block = lax.axis_index("obs")
    part = unit // subs
    units = pieces[0].shape[0] // part
    for a in range(position.shape[0]):
        position[a] = -1
    for k in range(listed):
        position[info[k]] = k
    for step, piece in enumerate(pieces):
        for u in range(units):
            row = ((block ^ step) * units + u) * unit
            at = position[row // tile]

            @pl.when(at >= 0)
            def _():
                first = pl.multiple_of(at * (tile // subs) + (row % tile) // subs, part)
                out[pl.ds(first, part), :] = piece[u * part:(u + 1) * part, :]


def product_kernel(unit, subs, held, weighted, *refs):
    pieces, outs = refs[:subs], refs[subs:2 * subs]
    probe, product = refs[2 * subs:]
    sub = lax.axis_index("sub")
    width = held.shape[1]
    part = unit // subs
    for j in range(subs):
        for g in range(width // unit):
            first = pl.multiple_of(g * unit + (sub ^ j) * part, part)
            probe[pl.ds(first, part), :] = pieces[j][g * part:(g + 1) * part, :]
    image = jnp.dot(held[...], probe[...], preferred_element_type=jnp.float32)
    image_t = image.astype(jnp.bfloat16).T
    product[...] = jnp.dot(image_t, weighted[...], preferred_element_type=jnp.float32)
    high = product.shape[0] // subs
    for j in range(subs):
        first = pl.multiple_of((sub ^ j) * high, high)
        outs[j][...] = product[pl.ds(first, high), :].astype(outs[j].dtype)


def place_kernel(unit, tile, listed, parts_count, info, *refs):
    parts, outs = refs[:parts_count], refs[parts_count:-2]
    position, total = refs[-2:]
    block = lax.axis_index("obs")
    for a in range(position.shape[0]):
        position[a] = -1
    for k in range(listed):
        position[info[listed + info[k]]] = k
    value = parts[0][...]
    for term in parts[1:]:
        value = value + term[...].astype(jnp.float32)
    total[...] = value
    units = outs[0].shape[1] // unit
    for step, out in enumerate(outs):
        for u in range(units):
            row = ((block ^ step) * units + u) * unit
            at = position[row // tile]
            first = pl.multiple_of(jnp.maximum(at, 0) * tile, tile)
            whole = jnp.where(at >= 0, total[:, pl.ds(first, tile)], 0.0)
            taken = whole[:, :unit]
            for q in range(1, tile // unit):
                taken = jnp.where(row % tile == q * unit, whole[:, q * unit:(q + 1) * unit], taken)
            out[:, u * unit:(u + 1) * unit] = taken.astype(out.dtype)


def kept(step):
    return jnp.float32 if step % 2 == 0 else jnp.bfloat16


def local(obs_count, subs, jacobian, obs_weight, row_counts, tile_lists, tile_slot, probe_block):
    rows, width = jacobian.shape
    tiles = tile_slot.shape[0]
    listed = tile_lists.shape[1]
    tile = width // listed
    own_rows, probe_width = probe_block.shape
    unit = min(own_rows, tile)
    high = probe_width // subs
    my_list = lax.dynamic_index_in_dim(tile_lists, lax.axis_index("obs"), 0, keepdims=False)
    info = jnp.concatenate([my_list, tile_slot])

    def params(mib):
        return pltpu.CompilerParams(vmem_limit_bytes=mib * MIB)

    share = pl.pallas_call(
        functools.partial(share_kernel, unit, subs),
        out_shape=jax.ShapeDtypeStruct((own_rows // subs, probe_width), jnp.bfloat16),
        in_specs=[HBM],
        out_specs=VMEM,
        scratch_shapes=[pltpu.SemaphoreType.DMA((own_rows // unit,))],
        compiler_params=params(60),
        name="share_probe",
    )(probe_block)
    weight_lanes = min(128, rows)
    held, weighted = pl.pallas_call(
        weigh_kernel,
        out_shape=[jax.ShapeDtypeStruct((rows, width), jnp.bfloat16)] * 2,
        in_specs=[SMEM, VMEM, HBM],
        out_specs=[VMEM, VMEM],
        scratch_shapes=[pltpu.SemaphoreType.DMA((4,))],
        compiler_params=params(16),
        cost_estimate=pl.CostEstimate(flops=2 * rows * width, bytes_accessed=6 * rows * width, transcendentals=0),
        name="weigh",
    )(row_counts, obs_weight.reshape(rows // weight_lanes, weight_lanes), jacobian)

    pick = pl.pallas_call(
        functools.partial(pick_kernel, unit, tile, subs, listed),
        out_shape=jax.ShapeDtypeStruct((width // subs, probe_width), jnp.bfloat16),
        in_specs=[SMEM, pl.BlockSpec(memory_space=pl.ANY)] + [VMEM] * obs_count,
        out_specs=VMEM,
        scratch_shapes=[pltpu.SMEM((tiles,), jnp.int32)],
        compiler_params=params(8),
        name="pick_listed",
    )
    product = pl.pallas_call(
        functools.partial(product_kernel, unit, subs),
        out_shape=[jax.ShapeDtypeStruct((high, width), kept(j)) for j in range(subs)],
        in_specs=[VMEM] * (2 + subs),
        out_specs=[VMEM] * subs,
        scratch_shapes=[
            pltpu.VMEM((width, probe_width), jnp.bfloat16),
            pltpu.VMEM((probe_width, width), jnp.float32),
        ],
        compiler_params=params(24),
        cost_estimate=pl.CostEstimate(
            flops=4 * rows * width * probe_width, bytes_accessed=4 * rows * width, transcendentals=0),
        name="product",
    )
    place = pl.pallas_call(
        functools.partial(place_kernel, unit, tile, listed, subs // 2 + 1),
        out_shape=[jax.ShapeDtypeStruct((high, own_rows), kept(step)) for step in range(obs_count)],
        in_specs=[SMEM] + [VMEM] * (subs // 2 + 1),
        out_specs=[VMEM] * obs_count,
        scratch_shapes=[pltpu.SMEM((tiles,), jnp.int32), pltpu.VMEM((high, width), jnp.float32)],
        compiler_params=params(8),
        name="place",
    )

    pieces = spread(share, "obs", obs_count)
    columns = spread(pick(info, weighted, *pieces), "sub", subs)
    terms = collect(product(held, weighted, *columns), "sub", subs)
    terms = collect(place(info, *terms), "obs", obs_count)
    return sum(term.astype(jnp.float32) for term in terms).T.astype(jnp.bfloat16)


def solution(mesh):
    placed = (P(("obs", "sub"), None), P(("obs", "sub")), P("obs"), P(), P(), P("obs", None))
    return jax.shard_map(
        functools.partial(local, mesh.shape["obs"], mesh.shape["sub"]),
        mesh=mesh, in_specs=placed, out_specs=P("obs", "sub"), check_vma=False,
    )
```

```python
import functools

import jax
import jax.numpy as jnp
from jax import lax
from jax.experimental import pallas as pl
from jax.experimental.pallas import tpu as pltpu
from jax.sharding import PartitionSpec as P

MIB = 1024 * 1024
SUB_DIRECT = 2
OBS_DIRECT = 4
COLUMNS = 512
SMEM = pl.BlockSpec(memory_space=pltpu.SMEM)
VMEM = pl.BlockSpec(memory_space=pltpu.VMEM)
HBM = pl.BlockSpec(memory_space=pltpu.HBM)


def swap(value, axis, count, step):
    return lax.ppermute(value, axis, [(i, i ^ step) for i in range(count)])


def far_steps(count):
    return [2 * high for high in range(count // 2 - 1, 0, -1)]


def spread(value, axis, count, before=None):
    held = {0: value}
    for step in far_steps(count):
        held[step] = swap(value, axis, count, step)
    held[1] = swap(value, axis, count, 1)
    for step in far_steps(count):
        passed = held[step] if before is None else lax.optimization_barrier((held[step], before))[0]
        held[step + 1] = swap(passed, axis, count, 1)
    return [held[step] for step in range(count)]


def collect(terms, axis, count, direct):
    parts = [terms[0]]
    for step in range(count - 2, direct - 1, -2):
        passed = swap(terms[step + 1], axis, count, 1)
        both = (terms[step] + passed.astype(jnp.float32)).astype(jnp.bfloat16)
        parts.append(swap(both, axis, count, step))
    for step in range(min(direct, count) - 1, 0, -1):
        parts.append(swap(terms[step], axis, count, step))
    return parts


def weigh_kernel(count, weight, jac, after, held, weighted, sems):
    rows, width = held.shape
    chunk = rows // sems.shape[0]
    copies = [
        pltpu.make_async_copy(jac.at[pl.ds(i * chunk, chunk)], held.at[pl.ds(i * chunk, chunk)], sems.at[i])
        for i in range(sems.shape[0])
    ]
    for copy in copies:
        copy.start()
    sub = lax.axis_index("sub")
    lanes = weight.shape[1]
    for i, copy in enumerate(copies):
        copy.wait()
        for r in range(i * chunk, (i + 1) * chunk, lanes):
            at = sub * rows + r + lax.broadcasted_iota(jnp.int32, (lanes, lanes), 0)
            scale = jnp.broadcast_to(weight[r // lanes:r // lanes + 1, :], (lanes, lanes)).T
            scale = scale * (at < count[0]).astype(jnp.float32)
            scale = jnp.concatenate([scale] * (width // lanes), axis=1)
            weighted[r:r + lanes, :] = (held[r:r + lanes, :].astype(jnp.float32) * scale).astype(jnp.bfloat16)


def pick_kernel(unit, tile, subs, listed, info, *refs):
    pieces, out, position = refs[:-2], refs[-2], refs[-1]
    block = lax.axis_index("obs")
    part = unit // subs
    units = pieces[0].shape[0] // part
    for a in range(position.shape[0]):
        position[a] = -1
    for k in range(listed):
        position[info[k]] = k
    for step, piece in enumerate(pieces):
        for u in range(units):
            row = ((block ^ step) * units + u) * unit
            at = position[row // tile]

            @pl.when(at >= 0)
            def _():
                first = pl.multiple_of(at * (tile // subs) + (row % tile) // subs, part)
                out[pl.ds(first, part), :] = piece[u * part:(u + 1) * part, :]


def product_kernel(unit, subs, held, weighted, *refs):
    pieces, outs = refs[:subs], refs[subs:2 * subs]
    probe, image_t = refs[2 * subs:]
    sub = lax.axis_index("sub")
    width = held.shape[1]
    part = unit // subs
    for j in range(subs):
        for g in range(width // unit):
            first = pl.multiple_of(g * unit + (sub ^ j) * part, part)
            probe[pl.ds(first, part), :] = pieces[j][g * part:(g + 1) * part, :]
    image = jnp.dot(held[...], probe[...], preferred_element_type=jnp.float32)
    image_t[...] = image.astype(jnp.bfloat16).T
    high = image_t.shape[0] // subs
    by_step = [image_t[pl.ds(pl.multiple_of((sub ^ j) * high, high), high), :] for j in range(subs)]
    by_step = jnp.concatenate(by_step, axis=0)
    for n in range(0, width, COLUMNS):
        product = jnp.dot(by_step, weighted[:, n:n + COLUMNS], preferred_element_type=jnp.float32)
        for j in range(subs):
            outs[j][:, n:n + COLUMNS] = product[j * high:(j + 1) * high, :].astype(outs[j].dtype)


def place_kernel(unit, tile, listed, parts_count, info, *refs):
    parts, outs = refs[:parts_count], refs[parts_count:-2]
    position, total = refs[-2:]
    block = lax.axis_index("obs")
    for a in range(position.shape[0]):
        position[a] = -1
    for k in range(listed):
        position[info[listed + info[k]]] = k
    value = parts[0][...]
    for term in parts[1:]:
        value = value + term[...].astype(jnp.float32)
    total[...] = value
    units = outs[0].shape[1] // unit
    for step, out in enumerate(outs):
        for u in range(units):
            row = ((block ^ step) * units + u) * unit
            at = position[row // tile]
            first = pl.multiple_of(jnp.maximum(at, 0) * tile, tile)
            whole = jnp.where(at >= 0, total[:, pl.ds(first, tile)], 0.0)
            taken = whole[:, :unit]
            for q in range(1, tile // unit):
                taken = jnp.where(row % tile == q * unit, whole[:, q * unit:(q + 1) * unit], taken)
            out[:, u * unit:(u + 1) * unit] = taken.astype(out.dtype)


def kept(step, direct):
    return jnp.float32 if step == 0 or step >= direct and step % 2 == 0 else jnp.bfloat16


def local(obs_count, subs, jacobian, obs_weight, row_counts, tile_lists, tile_slot, probe_block):
    rows, width = jacobian.shape
    tiles = tile_slot.shape[0]
    listed = tile_lists.shape[1]
    tile = width // listed
    own_rows, probe_width = probe_block.shape
    unit = min(own_rows, tile)
    high = probe_width // subs
    my_list = lax.dynamic_index_in_dim(tile_lists, lax.axis_index("obs"), 0, keepdims=False)
    info = jnp.concatenate([my_list, tile_slot])

    def params(mib):
        return pltpu.CompilerParams(vmem_limit_bytes=mib * MIB)

    share = probe_block.reshape(own_rows // unit, subs, unit // subs, probe_width)
    share = lax.dynamic_index_in_dim(share, lax.axis_index("sub"), 1, keepdims=False)
    share = share.reshape(own_rows // subs, probe_width)
    pick = pl.pallas_call(
        functools.partial(pick_kernel, unit, tile, subs, listed),
        out_shape=jax.ShapeDtypeStruct((width // subs, probe_width), jnp.bfloat16),
        in_specs=[SMEM] + [VMEM] * obs_count,
        out_specs=VMEM,
        scratch_shapes=[pltpu.SMEM((tiles,), jnp.int32)],
        compiler_params=params(8),
        name="pick_listed",
    )
    picked = pick(info, *spread(share, "obs", obs_count))
    weight_lanes = min(128, rows)
    held, weighted = pl.pallas_call(
        weigh_kernel,
        out_shape=[jax.ShapeDtypeStruct((rows, width), jnp.bfloat16)] * 2,
        in_specs=[SMEM, VMEM, HBM, pl.BlockSpec(memory_space=pl.ANY)],
        out_specs=[VMEM, VMEM],
        scratch_shapes=[pltpu.SemaphoreType.DMA((4,))],
        compiler_params=params(16),
        cost_estimate=pl.CostEstimate(flops=2 * rows * width, bytes_accessed=6 * rows * width, transcendentals=0),
        name="weigh",
    )(row_counts, obs_weight.reshape(rows // weight_lanes, weight_lanes), jacobian, picked)

    product = pl.pallas_call(
        functools.partial(product_kernel, unit, subs),
        out_shape=[jax.ShapeDtypeStruct((high, width), kept(j, SUB_DIRECT)) for j in range(subs)],
        in_specs=[VMEM] * (2 + subs),
        out_specs=[VMEM] * subs,
        scratch_shapes=[
            pltpu.VMEM((width, probe_width), jnp.bfloat16),
            pltpu.VMEM((probe_width, rows), jnp.bfloat16),
        ],
        compiler_params=params(24),
        cost_estimate=pl.CostEstimate(
            flops=4 * rows * width * probe_width, bytes_accessed=4 * rows * width, transcendentals=0),
        name="product",
    )
    place = pl.pallas_call(
        functools.partial(place_kernel, unit, tile, listed, subs // 2 + 1),
        out_shape=[jax.ShapeDtypeStruct((high, own_rows), kept(step, OBS_DIRECT)) for step in range(obs_count)],
        in_specs=[SMEM] + [VMEM] * (subs // 2 + 1),
        out_specs=[VMEM] * obs_count,
        scratch_shapes=[pltpu.SMEM((tiles,), jnp.int32), pltpu.VMEM((high, width), jnp.float32)],
        compiler_params=params(8),
        name="place",
    )

    columns = spread(picked, "sub", subs, weighted)
    terms = collect(product(held, weighted, *columns), "sub", subs, SUB_DIRECT)
    terms = collect(place(info, *terms), "obs", obs_count, OBS_DIRECT)
    return sum(term.astype(jnp.float32) for term in terms).T.astype(jnp.bfloat16)


def solution(mesh):
    placed = (P(("obs", "sub"), None), P(("obs", "sub")), P("obs"), P(), P(), P("obs", None))
    return jax.shard_map(
        functools.partial(local, mesh.shape["obs"], mesh.shape["sub"]),
        mesh=mesh, in_specs=placed, out_specs=P("obs", "sub"), check_vma=False,
    )
```

```python
import functools

import jax
import jax.numpy as jnp
from jax import lax
from jax.experimental import pallas as pl
from jax.experimental.pallas import tpu as pltpu
from jax.sharding import PartitionSpec as P

MIB = 1024 * 1024
SUB_DIRECT = 2
OBS_DIRECT = 4
COLUMNS = 512
CONTRACT_LAST = (((1,), (1,)), ((), ()))
SMEM = pl.BlockSpec(memory_space=pltpu.SMEM)
VMEM = pl.BlockSpec(memory_space=pltpu.VMEM)
HBM = pl.BlockSpec(memory_space=pltpu.HBM)


def swap(value, axis, count, step):
    return lax.ppermute(value, axis, [(i, i ^ step) for i in range(count)])


def after(value, *before):
    return lax.optimization_barrier((value, *before))[0]


def spread(value, axis, count, direct, before=()):
    held = {0: value}
    far = range(count - 2, direct - 1, -2)
    for step in (*far, *range(min(direct, count) - 1, 0, -1)):
        held[step] = swap(value, axis, count, step)
    for step in far:
        held[step + 1] = swap(after(held[step], *before), axis, count, 1)
    return [held[step] for step in range(count)]


def collect(terms, axis, count, direct):
    parts, both = [terms[0]], []
    far = range(count - 2, direct - 1, -2)
    passed = [swap(terms[step + 1], axis, count, 1) for step in far]
    parts.append(swap(terms[1], axis, count, 1))
    for step, part in zip(far, passed):
        both.append((terms[step] + part.astype(jnp.float32)).astype(jnp.bfloat16))
        parts.append(swap(both[-1], axis, count, step))
    for step in range(min(direct, count) - 1, 1, -1):
        parts.append(swap(after(terms[step], *both), axis, count, step))
    return parts


def share_kernel(probe, out):
    high, width = out.shape[0], probe.shape[1]
    first = lax.axis_index("sub") * high
    row = lax.broadcasted_iota(jnp.int32, (high, width), 0)
    column = lax.broadcasted_iota(jnp.int32, (high, width), 1)
    wanted = (column == row + first).astype(jnp.bfloat16)
    out[...] = lax.dot_general(wanted, probe[...], CONTRACT_LAST, preferred_element_type=jnp.float32).astype(out.dtype)


def weigh_kernel(count, weight, jac, after, held, weighted, sems):
    rows, width = held.shape
    chunk = rows // sems.shape[0]
    copies = [
        pltpu.make_async_copy(jac.at[pl.ds(i * chunk, chunk)], held.at[pl.ds(i * chunk, chunk)], sems.at[i])
        for i in range(sems.shape[0])
    ]
    for copy in copies:
        copy.start()
    sub = lax.axis_index("sub")
    lanes = weight.shape[1]
    for i, copy in enumerate(copies):
        copy.wait()
        for r in range(i * chunk, (i + 1) * chunk, lanes):
            at = sub * rows + r + lax.broadcasted_iota(jnp.int32, (lanes, lanes), 0)
            scale = jnp.broadcast_to(weight[r // lanes:r // lanes + 1, :], (lanes, lanes)).T
            scale = scale * (at < count[0]).astype(jnp.float32)
            scale = jnp.concatenate([scale] * (width // lanes), axis=1)
            weighted[r:r + lanes, :] = (held[r:r + lanes, :].astype(jnp.float32) * scale).astype(jnp.bfloat16)


def pick_kernel(unit, info, *refs):
    pieces, out, position = refs[:-2], refs[-2], refs[-1]
    listed, _, tile = out.shape
    block = lax.axis_index("obs")
    units = pieces[0].shape[1] // unit
    for a in range(position.shape[0]):
        position[a] = -1
    for k in range(listed):
        position[info[k]] = k
    for step, piece in enumerate(pieces):
        for u in range(units):
            row = ((block ^ step) * units + u) * unit
            at = position[row // tile]
            for q in range(tile // unit):

                @pl.when((at >= 0) & (row % tile == q * unit))
                def _():
                    out[at, :, q * unit:(q + 1) * unit] = piece[:, u * unit:(u + 1) * unit]


def product_kernel(held, weighted, *refs):
    pieces, outs, probe = refs[:len(refs) // 2], refs[len(refs) // 2:-1], refs[-1]
    listed, high, tile = pieces[0].shape
    for j, piece in enumerate(pieces):
        for k in range(listed):
            probe[j * high:(j + 1) * high, k * tile:(k + 1) * tile] = piece[k]
    image = lax.dot_general(probe[...], held[...], CONTRACT_LAST, preferred_element_type=jnp.float32)
    image = image.astype(jnp.bfloat16)
    for n in range(0, held.shape[1], COLUMNS):
        product = jnp.dot(image, weighted[:, n:n + COLUMNS], preferred_element_type=jnp.float32)
        for j, out in enumerate(outs):
            out[:, n:n + COLUMNS] = product[j * high:(j + 1) * high, :].astype(out.dtype)


def place_kernel(unit, tile, listed, parts_count, info, *refs):
    parts, outs = refs[:parts_count], refs[parts_count:-2]
    position, total = refs[-2:]
    block = lax.axis_index("obs")
    for a in range(position.shape[0]):
        position[a] = -1
    for k in range(listed):
        position[info[listed + info[k]]] = k
    value = parts[0][...]
    for term in parts[1:]:
        value = value + term[...].astype(jnp.float32)
    total[...] = value
    units = outs[0].shape[1] // unit
    for step, out in enumerate(outs):
        for u in range(units):
            row = ((block ^ step) * units + u) * unit
            at = position[row // tile]
            first = pl.multiple_of(jnp.maximum(at, 0) * tile, tile)
            whole = jnp.where(at >= 0, total[:, pl.ds(first, tile)], 0.0)
            taken = whole[:, :unit]
            for q in range(1, tile // unit):
                taken = jnp.where(row % tile == q * unit, whole[:, q * unit:(q + 1) * unit], taken)
            out[:, u * unit:(u + 1) * unit] = taken.astype(out.dtype)


def kept(step, direct):
    return jnp.float32 if step == 0 or step >= direct and step % 2 == 0 else jnp.bfloat16


def local(obs_count, subs, jacobian, obs_weight, row_counts, tile_lists, tile_slot, probe_block):
    rows, width = jacobian.shape
    tiles = tile_slot.shape[0]
    listed = tile_lists.shape[1]
    tile = width // listed
    own_rows, probe_width = probe_block.shape
    unit = min(own_rows, tile)
    high = probe_width // subs
    my_list = lax.dynamic_index_in_dim(tile_lists, lax.axis_index("obs"), 0, keepdims=False)
    info = jnp.concatenate([my_list, tile_slot])

    def params(mib):
        return pltpu.CompilerParams(vmem_limit_bytes=mib * MIB)

    share = pl.pallas_call(
        share_kernel,
        out_shape=jax.ShapeDtypeStruct((high, own_rows), jnp.bfloat16),
        in_specs=[VMEM],
        out_specs=VMEM,
        compiler_params=params(8),
        name="share_probe",
    )(probe_block)
    pick = pl.pallas_call(
        functools.partial(pick_kernel, unit),
        out_shape=jax.ShapeDtypeStruct((listed, high, tile), jnp.bfloat16),
        in_specs=[SMEM] + [VMEM] * obs_count,
        out_specs=VMEM,
        scratch_shapes=[pltpu.SMEM((tiles,), jnp.int32)],
        compiler_params=params(8),
        name="pick_listed",
    )
    picked = pick(info, *spread(share, "obs", obs_count, OBS_DIRECT))
    weight_lanes = min(128, rows)
    held, weighted = pl.pallas_call(
        weigh_kernel,
        out_shape=[jax.ShapeDtypeStruct((rows, width), jnp.bfloat16)] * 2,
        in_specs=[SMEM, VMEM, HBM, pl.BlockSpec(memory_space=pl.ANY)],
        out_specs=[VMEM, VMEM],
        scratch_shapes=[pltpu.SemaphoreType.DMA((4,))],
        compiler_params=params(16),
        cost_estimate=pl.CostEstimate(flops=2 * rows * width, bytes_accessed=6 * rows * width, transcendentals=0),
        name="weigh",
    )(row_counts, obs_weight.reshape(rows // weight_lanes, weight_lanes), jacobian, picked)

    product = pl.pallas_call(
        product_kernel,
        out_shape=[jax.ShapeDtypeStruct((high, width), kept(j, SUB_DIRECT)) for j in range(subs)],
        in_specs=[VMEM] * (2 + subs),
        out_specs=[VMEM] * subs,
        scratch_shapes=[
            pltpu.VMEM((probe_width, width), jnp.bfloat16),
        ],
        compiler_params=params(24),
        cost_estimate=pl.CostEstimate(
            flops=4 * rows * width * probe_width, bytes_accessed=4 * rows * width, transcendentals=0),
        name="product",
    )
    place = pl.pallas_call(
        functools.partial(place_kernel, unit, tile, listed, subs // 2 + 1),
        out_shape=[jax.ShapeDtypeStruct((high, own_rows), kept(step, OBS_DIRECT)) for step in range(obs_count)],
        in_specs=[SMEM] + [VMEM] * (subs // 2 + 1),
        out_specs=[VMEM] * obs_count,
        scratch_shapes=[pltpu.SMEM((tiles,), jnp.int32), pltpu.VMEM((high, width), jnp.float32)],
        compiler_params=params(8),
        name="place",
    )

    columns = spread(picked, "sub", subs, SUB_DIRECT, (weighted,))
    terms = collect(product(held, weighted, *columns), "sub", subs, SUB_DIRECT)
    terms = collect(place(info, *terms), "obs", obs_count, OBS_DIRECT)
    return sum(term.astype(jnp.float32) for term in terms).T.astype(jnp.bfloat16)


def solution(mesh):
    placed = (P(("obs", "sub"), None), P(("obs", "sub")), P("obs"), P(), P(), P("obs", None))
    return jax.shard_map(
        functools.partial(local, mesh.shape["obs"], mesh.shape["sub"]),
        mesh=mesh, in_specs=placed, out_specs=P("obs", "sub"), check_vma=False,
    )
```

```python
import functools

import jax
import jax.numpy as jnp
from jax import lax
from jax.experimental import pallas as pl
from jax.experimental.pallas import tpu as pltpu
from jax.sharding import PartitionSpec as P

MIB = 1024 * 1024
SPREAD_DIRECT = 2
SUB_DIRECT = 2
OBS_DIRECT = 4
COLUMNS = 512
CONTRACT_LAST = (((1,), (1,)), ((), ()))
SMEM = pl.BlockSpec(memory_space=pltpu.SMEM)
VMEM = pl.BlockSpec(memory_space=pltpu.VMEM)
HBM = pl.BlockSpec(memory_space=pltpu.HBM)


def swap(value, axis, count, step):
    return lax.ppermute(value, axis, [(i, i ^ step) for i in range(count)])


def after(value, *before):
    return lax.optimization_barrier((value, *before))[0]


def spread(value, axis, count, direct, before=()):
    held = {0: value}
    far = range(count - 2, direct - 1, -2)
    for step in (*far, *range(min(direct, count) - 1, 0, -1)):
        held[step] = swap(value, axis, count, step)
    for step in far:
        held[step + 1] = swap(after(held[step], *before), axis, count, 1)
    return [held[step] for step in range(count)]


def collect(terms, axis, count, direct):
    parts = [terms[0]]
    for step in range(count - 2, direct - 1, -2):
        passed = swap(terms[step + 1], axis, count, 1)
        both = (terms[step] + passed.astype(jnp.float32)).astype(jnp.bfloat16)
        parts.append(swap(both, axis, count, step))
    for step in range(min(direct, count) - 1, 0, -1):
        parts.append(swap(terms[step], axis, count, step))
    return parts


def share_kernel(probe, out):
    high, width = out.shape[0], probe.shape[1]
    first = lax.axis_index("sub") * high
    row = lax.broadcasted_iota(jnp.int32, (high, width), 0)
    column = lax.broadcasted_iota(jnp.int32, (high, width), 1)
    wanted = (column == row + first).astype(jnp.bfloat16)
    out[...] = lax.dot_general(wanted, probe[...], CONTRACT_LAST, preferred_element_type=jnp.float32).astype(out.dtype)


def weigh_kernel(count, weight, jac, after, held, weighted, sems):
    rows, width = held.shape
    chunk = rows // sems.shape[0]
    copies = [
        pltpu.make_async_copy(jac.at[pl.ds(i * chunk, chunk)], held.at[pl.ds(i * chunk, chunk)], sems.at[i])
        for i in range(sems.shape[0])
    ]
    for copy in copies:
        copy.start()
    sub = lax.axis_index("sub")
    lanes = weight.shape[1]
    for i, copy in enumerate(copies):
        copy.wait()
        for r in range(i * chunk, (i + 1) * chunk, lanes):
            at = sub * rows + r + lax.broadcasted_iota(jnp.int32, (lanes, lanes), 0)
            scale = jnp.broadcast_to(weight[r // lanes:r // lanes + 1, :], (lanes, lanes)).T
            scale = scale * (at < count[0]).astype(jnp.float32)
            scale = jnp.concatenate([scale] * (width // lanes), axis=1)
            weighted[r:r + lanes, :] = (held[r:r + lanes, :].astype(jnp.float32) * scale).astype(jnp.bfloat16)


def pick_kernel(unit, info, *refs):
    pieces, out, position = refs[:-2], refs[-2], refs[-1]
    listed, _, tile = out.shape
    block = lax.axis_index("obs")
    units = pieces[0].shape[1] // unit
    for a in range(position.shape[0]):
        position[a] = -1
    for k in range(listed):
        position[info[k]] = k
    for step, piece in enumerate(pieces):
        for u in range(units):
            row = ((block ^ step) * units + u) * unit
            at = position[row // tile]
            for q in range(tile // unit):

                @pl.when((at >= 0) & (row % tile == q * unit))
                def _():
                    out[at, :, q * unit:(q + 1) * unit] = piece[:, u * unit:(u + 1) * unit]


def product_kernel(held, weighted, *refs):
    pieces, outs, probe = refs[:len(refs) // 2], refs[len(refs) // 2:-1], refs[-1]
    listed, high, tile = pieces[0].shape
    for j, piece in enumerate(pieces):
        for k in range(listed):
            probe[j * high:(j + 1) * high, k * tile:(k + 1) * tile] = piece[k]
    image = lax.dot_general(probe[...], held[...], CONTRACT_LAST, preferred_element_type=jnp.float32)
    image = image.astype(jnp.bfloat16)
    for n in range(0, held.shape[1], COLUMNS):
        product = jnp.dot(image, weighted[:, n:n + COLUMNS], preferred_element_type=jnp.float32)
        for j, out in enumerate(outs):
            out[:, n:n + COLUMNS] = product[j * high:(j + 1) * high, :].astype(out.dtype)


def place_kernel(unit, tile, listed, parts_count, info, *refs):
    parts, outs = refs[:parts_count], refs[parts_count:-2]
    position, total = refs[-2:]
    block = lax.axis_index("obs")
    for a in range(position.shape[0]):
        position[a] = -1
    for k in range(listed):
        position[info[listed + info[k]]] = k
    value = parts[0][...]
    for term in parts[1:]:
        value = value + term[...].astype(jnp.float32)
    total[...] = value
    units = outs[0].shape[1] // unit
    for step, out in enumerate(outs):
        for u in range(units):
            row = ((block ^ step) * units + u) * unit
            at = position[row // tile]
            first = pl.multiple_of(jnp.maximum(at, 0) * tile, tile)
            whole = jnp.where(at >= 0, total[:, pl.ds(first, tile)], 0.0)
            taken = whole[:, :unit]
            for q in range(1, tile // unit):
                taken = jnp.where(row % tile == q * unit, whole[:, q * unit:(q + 1) * unit], taken)
            out[:, u * unit:(u + 1) * unit] = taken.astype(out.dtype)


def kept(step, direct):
    return jnp.float32 if step == 0 or step >= direct and step % 2 == 0 else jnp.bfloat16


def local(obs_count, subs, jacobian, obs_weight, row_counts, tile_lists, tile_slot, probe_block):
    rows, width = jacobian.shape
    tiles = tile_slot.shape[0]
    listed = tile_lists.shape[1]
    tile = width // listed
    own_rows, probe_width = probe_block.shape
    unit = min(own_rows, tile)
    high = probe_width // subs
    my_list = lax.dynamic_index_in_dim(tile_lists, lax.axis_index("obs"), 0, keepdims=False)
    info = jnp.concatenate([my_list, tile_slot])

    def params(mib):
        return pltpu.CompilerParams(vmem_limit_bytes=mib * MIB)

    share = pl.pallas_call(
        share_kernel,
        out_shape=jax.ShapeDtypeStruct((high, own_rows), jnp.bfloat16),
        in_specs=[VMEM],
        out_specs=VMEM,
        compiler_params=params(8),
        name="share_probe",
    )(probe_block)
    pick = pl.pallas_call(
        functools.partial(pick_kernel, unit),
        out_shape=jax.ShapeDtypeStruct((listed, high, tile), jnp.bfloat16),
        in_specs=[SMEM] + [VMEM] * obs_count,
        out_specs=VMEM,
        scratch_shapes=[pltpu.SMEM((tiles,), jnp.int32)],
        compiler_params=params(8),
        name="pick_listed",
    )
    picked = pick(info, *spread(share, "obs", obs_count, SPREAD_DIRECT))
    weight_lanes = min(128, rows)
    held, weighted = pl.pallas_call(
        weigh_kernel,
        out_shape=[jax.ShapeDtypeStruct((rows, width), jnp.bfloat16)] * 2,
        in_specs=[SMEM, VMEM, HBM, pl.BlockSpec(memory_space=pl.ANY)],
        out_specs=[VMEM, VMEM],
        scratch_shapes=[pltpu.SemaphoreType.DMA((4,))],
        compiler_params=params(16),
        cost_estimate=pl.CostEstimate(flops=2 * rows * width, bytes_accessed=6 * rows * width, transcendentals=0),
        name="weigh",
    )(row_counts, obs_weight.reshape(rows // weight_lanes, weight_lanes), jacobian, picked)

    product = pl.pallas_call(
        product_kernel,
        out_shape=[jax.ShapeDtypeStruct((high, width), kept(j, SUB_DIRECT)) for j in range(subs)],
        in_specs=[VMEM] * (2 + subs),
        out_specs=[VMEM] * subs,
        scratch_shapes=[
            pltpu.VMEM((probe_width, width), jnp.bfloat16),
        ],
        compiler_params=params(24),
        cost_estimate=pl.CostEstimate(
            flops=4 * rows * width * probe_width, bytes_accessed=4 * rows * width, transcendentals=0),
        name="product",
    )
    place = pl.pallas_call(
        functools.partial(place_kernel, unit, tile, listed, subs // 2 + 1),
        out_shape=[jax.ShapeDtypeStruct((high, own_rows), kept(step, OBS_DIRECT)) for step in range(obs_count)],
        in_specs=[SMEM] + [VMEM] * (subs // 2 + 1),
        out_specs=[VMEM] * obs_count,
        scratch_shapes=[pltpu.SMEM((tiles,), jnp.int32), pltpu.VMEM((high, width), jnp.float32)],
        compiler_params=params(8),
        name="place",
    )

    columns = spread(picked, "sub", subs, SPREAD_DIRECT, (weighted,))
    terms = collect(product(held, weighted, *columns), "sub", subs, SUB_DIRECT)
    terms = collect(place(info, *terms), "obs", obs_count, OBS_DIRECT)
    return sum(term.astype(jnp.float32) for term in terms).T.astype(jnp.bfloat16)


def solution(mesh):
    placed = (P(("obs", "sub"), None), P(("obs", "sub")), P("obs"), P(), P(), P("obs", None))
    return jax.shard_map(
        functools.partial(local, mesh.shape["obs"], mesh.shape["sub"]),
        mesh=mesh, in_specs=placed, out_specs=P("obs", "sub"), check_vma=False,
    )
```

```python
import functools

import jax
import jax.numpy as jnp
from jax import lax
from jax.experimental import pallas as pl
from jax.experimental.pallas import tpu as pltpu
from jax.sharding import PartitionSpec as P

MIB = 1024 * 1024
SPREAD_DIRECT = 2
SUB_DIRECT = 2
OBS_DIRECT = 4
COLUMNS = 512
CONTRACT_LAST = (((1,), (1,)), ((), ()))
SMEM = pl.BlockSpec(memory_space=pltpu.SMEM)
VMEM = pl.BlockSpec(memory_space=pltpu.VMEM)
HBM = pl.BlockSpec(memory_space=pltpu.HBM)


def swap(value, axis, count, step):
    return lax.ppermute(value, axis, [(i, i ^ step) for i in range(count)])


def after(value, *before):
    return lax.optimization_barrier((value, *before))[0]


def spread(value, axis, count, direct, before=()):
    held = {0: value}
    far = range(count - 2, direct - 1, -2)
    for step in (*far, *range(min(direct, count) - 1, 0, -1)):
        held[step] = swap(value, axis, count, step)
    for step in far:
        held[step + 1] = swap(after(held[step], *before), axis, count, 1)
    return [held[step] for step in range(count)]


def collect(terms, axis, count, direct):
    first, later, ready = [terms[0]], [], ()
    for step in range(count - 2, direct - 1, -2):
        passed = swap(terms[step + 1], axis, count, 1)
        ready = (terms[step] + passed.astype(jnp.float32)).astype(jnp.bfloat16),
        first.append(swap(*ready, axis, count, step))
    first.append(swap(terms[1], axis, count, 1))
    for step in range(min(direct, count) - 1, 1, -1):
        later.append(swap(after(terms[step], *ready), axis, count, step))
    return first, later


def share_kernel(probe, out):
    high, width = out.shape[0], probe.shape[1]
    first = lax.axis_index("sub") * high
    row = lax.broadcasted_iota(jnp.int32, (high, width), 0)
    column = lax.broadcasted_iota(jnp.int32, (high, width), 1)
    wanted = (column == row + first).astype(jnp.bfloat16)
    out[...] = lax.dot_general(wanted, probe[...], CONTRACT_LAST, preferred_element_type=jnp.float32).astype(out.dtype)


def weigh_kernel(count, weight, jac, after, held, weighted, sems):
    rows, width = held.shape
    chunk = rows // sems.shape[0]
    copies = [
        pltpu.make_async_copy(jac.at[pl.ds(i * chunk, chunk)], held.at[pl.ds(i * chunk, chunk)], sems.at[i])
        for i in range(sems.shape[0])
    ]
    for copy in copies:
        copy.start()
    sub = lax.axis_index("sub")
    lanes = weight.shape[1]
    for i, copy in enumerate(copies):
        copy.wait()
        for r in range(i * chunk, (i + 1) * chunk, lanes):
            at = sub * rows + r + lax.broadcasted_iota(jnp.int32, (lanes, lanes), 0)
            scale = jnp.broadcast_to(weight[r // lanes:r // lanes + 1, :], (lanes, lanes)).T
            scale = scale * (at < count[0]).astype(jnp.float32)
            scale = jnp.concatenate([scale] * (width // lanes), axis=1)
            weighted[r:r + lanes, :] = (held[r:r + lanes, :].astype(jnp.float32) * scale).astype(jnp.bfloat16)


def pick_kernel(unit, info, *refs):
    pieces, out, position = refs[:-2], refs[-2], refs[-1]
    listed, _, tile = out.shape
    block = lax.axis_index("obs")
    units = pieces[0].shape[1] // unit
    for a in range(position.shape[0]):
        position[a] = -1
    for k in range(listed):
        position[info[k]] = k
    for step, piece in enumerate(pieces):
        for u in range(units):
            row = ((block ^ step) * units + u) * unit
            at = position[row // tile]
            for q in range(tile // unit):

                @pl.when((at >= 0) & (row % tile == q * unit))
                def _():
                    out[at, :, q * unit:(q + 1) * unit] = piece[:, u * unit:(u + 1) * unit]


def product_kernel(held, weighted, *refs):
    pieces, outs, probe = refs[:len(refs) // 2], refs[len(refs) // 2:-1], refs[-1]
    listed, high, tile = pieces[0].shape
    for j, piece in enumerate(pieces):
        for k in range(listed):
            probe[j * high:(j + 1) * high, k * tile:(k + 1) * tile] = piece[k]
    image = lax.dot_general(probe[...], held[...], CONTRACT_LAST, preferred_element_type=jnp.float32)
    image = image.astype(jnp.bfloat16)
    for n in range(0, held.shape[1], COLUMNS):
        product = jnp.dot(image, weighted[:, n:n + COLUMNS], preferred_element_type=jnp.float32)
        for j, out in enumerate(outs):
            out[:, n:n + COLUMNS] = product[j * high:(j + 1) * high, :].astype(out.dtype)


def place_kernel(unit, tile, listed, parts_count, info, *refs):
    parts, outs = refs[:parts_count], refs[parts_count:-2]
    position, total = refs[-2:]
    block = lax.axis_index("obs")
    for a in range(position.shape[0]):
        position[a] = -1
    for k in range(listed):
        position[info[listed + info[k]]] = k
    value = parts[0][...]
    for term in parts[1:]:
        value = value + term[...].astype(jnp.float32)
    total[...] = value
    units = outs[0].shape[1] // unit
    for step, out in enumerate(outs):
        for u in range(units):
            row = ((block ^ step) * units + u) * unit
            at = position[row // tile]
            first = pl.multiple_of(jnp.maximum(at, 0) * tile, tile)
            whole = jnp.where(at >= 0, total[:, pl.ds(first, tile)], 0.0)
            taken = whole[:, :unit]
            for q in range(1, tile // unit):
                taken = jnp.where(row % tile == q * unit, whole[:, q * unit:(q + 1) * unit], taken)
            out[:, u * unit:(u + 1) * unit] = taken.astype(out.dtype)


def kept(step, direct):
    return jnp.float32 if step == 0 or step >= direct and step % 2 == 0 else jnp.bfloat16


def local(obs_count, subs, jacobian, obs_weight, row_counts, tile_lists, tile_slot, probe_block):
    rows, width = jacobian.shape
    tiles = tile_slot.shape[0]
    listed = tile_lists.shape[1]
    tile = width // listed
    own_rows, probe_width = probe_block.shape
    unit = min(own_rows, tile)
    high = probe_width // subs
    my_list = lax.dynamic_index_in_dim(tile_lists, lax.axis_index("obs"), 0, keepdims=False)
    info = jnp.concatenate([my_list, tile_slot])

    def params(mib):
        return pltpu.CompilerParams(vmem_limit_bytes=mib * MIB)

    share = pl.pallas_call(
        share_kernel,
        out_shape=jax.ShapeDtypeStruct((high, own_rows), jnp.bfloat16),
        in_specs=[VMEM],
        out_specs=VMEM,
        compiler_params=params(8),
        name="share_probe",
    )(probe_block)
    pick = pl.pallas_call(
        functools.partial(pick_kernel, unit),
        out_shape=jax.ShapeDtypeStruct((listed, high, tile), jnp.bfloat16),
        in_specs=[SMEM] + [VMEM] * obs_count,
        out_specs=VMEM,
        scratch_shapes=[pltpu.SMEM((tiles,), jnp.int32)],
        compiler_params=params(8),
        name="pick_listed",
    )
    picked = pick(info, *spread(share, "obs", obs_count, SPREAD_DIRECT))
    weight_lanes = min(128, rows)
    held, weighted = pl.pallas_call(
        weigh_kernel,
        out_shape=[jax.ShapeDtypeStruct((rows, width), jnp.bfloat16)] * 2,
        in_specs=[SMEM, VMEM, HBM, pl.BlockSpec(memory_space=pl.ANY)],
        out_specs=[VMEM, VMEM],
        scratch_shapes=[pltpu.SemaphoreType.DMA((4,))],
        compiler_params=params(16),
        cost_estimate=pl.CostEstimate(flops=2 * rows * width, bytes_accessed=6 * rows * width, transcendentals=0),
        name="weigh",
    )(row_counts, obs_weight.reshape(rows // weight_lanes, weight_lanes), jacobian, picked)

    product = pl.pallas_call(
        product_kernel,
        out_shape=[jax.ShapeDtypeStruct((high, width), kept(j, SUB_DIRECT)) for j in range(subs)],
        in_specs=[VMEM] * (2 + subs),
        out_specs=[VMEM] * subs,
        scratch_shapes=[
            pltpu.VMEM((probe_width, width), jnp.bfloat16),
        ],
        compiler_params=params(24),
        cost_estimate=pl.CostEstimate(
            flops=4 * rows * width * probe_width, bytes_accessed=4 * rows * width, transcendentals=0),
        name="product",
    )
    place = pl.pallas_call(
        functools.partial(place_kernel, unit, tile, listed, subs // 2 + 1),
        out_shape=[jax.ShapeDtypeStruct((high, own_rows), kept(step, OBS_DIRECT)) for step in range(obs_count)],
        in_specs=[SMEM] + [VMEM] * (subs // 2 + 1),
        out_specs=[VMEM] * obs_count,
        scratch_shapes=[pltpu.SMEM((tiles,), jnp.int32), pltpu.VMEM((high, width), jnp.float32)],
        compiler_params=params(8),
        name="place",
    )

    columns = spread(picked, "sub", subs, SPREAD_DIRECT, (weighted,))
    first, later = collect(product(held, weighted, *columns), "sub", subs, SUB_DIRECT)
    first, later = collect(place(info, *first, *later), "obs", obs_count, OBS_DIRECT)
    total = after(sum(term.astype(jnp.float32) for term in first))
    return sum((term.astype(jnp.float32) for term in later), total).T.astype(jnp.bfloat16)


def solution(mesh):
    placed = (P(("obs", "sub"), None), P(("obs", "sub")), P("obs"), P(), P(), P("obs", None))
    return jax.shard_map(
        functools.partial(local, mesh.shape["obs"], mesh.shape["sub"]),
        mesh=mesh, in_specs=placed, out_specs=P("obs", "sub"), check_vma=False,
    )
```

```python
import functools

import jax
import jax.numpy as jnp
from jax import lax
from jax.experimental import pallas as pl
from jax.experimental.pallas import tpu as pltpu
from jax.sharding import PartitionSpec as P

MIB = 1024 * 1024
SPREAD_DIRECT = 2
SUB_DIRECT = 2
OBS_DIRECT = 4
COLUMNS = 512
CONTRACT_LAST = (((1,), (1,)), ((), ()))
SMEM = pl.BlockSpec(memory_space=pltpu.SMEM)
VMEM = pl.BlockSpec(memory_space=pltpu.VMEM)
HBM = pl.BlockSpec(memory_space=pltpu.HBM)


def swap(value, axis, count, step):
    return lax.ppermute(value, axis, [(i, i ^ step) for i in range(count)])


def after(value, *before):
    return lax.optimization_barrier((value, *before))[0]


def spread(value, axis, count, direct, before=()):
    held = {0: value}
    far = range(count - 2, direct - 1, -2)
    for step in (*far, *range(min(direct, count) - 1, 0, -1)):
        held[step] = swap(value, axis, count, step)
    for step in far:
        held[step + 1] = swap(after(held[step], *before), axis, count, 1)
    return [held[step] for step in range(count)]


def collect(terms, axis, count, direct):
    first, later, ready = [terms[0]], [], ()
    for step in range(count - 2, direct - 1, -2):
        passed = swap(terms[step + 1], axis, count, 1)
        ready = (terms[step] + passed.astype(jnp.float32)).astype(jnp.bfloat16),
        first.append(swap(*ready, axis, count, step))
    first.append(swap(terms[1], axis, count, 1))
    for step in range(min(direct, count) - 1, 1, -1):
        if step % 2:
            later.append(swap(after(terms[step], *ready), axis, count, step))
        else:
            first.append(swap(terms[step], axis, count, step))
    return first, later


def share_kernel(probe, out):
    high, width = out.shape[0], probe.shape[1]
    first = lax.axis_index("sub") * high
    row = lax.broadcasted_iota(jnp.int32, (high, width), 0)
    column = lax.broadcasted_iota(jnp.int32, (high, width), 1)
    wanted = (column == row + first).astype(jnp.bfloat16)
    out[...] = lax.dot_general(wanted, probe[...], CONTRACT_LAST, preferred_element_type=jnp.float32).astype(out.dtype)


def weigh_kernel(weight, jac, after, weighted):
    rows, width = jac.shape
    lanes = weight.shape[1]
    for i in range(rows // lanes):
        scale = jnp.broadcast_to(weight[i:i + 1, :], (lanes, lanes)).T
        scale = jnp.concatenate([scale] * (width // lanes), axis=1)
        span = slice(i * lanes, (i + 1) * lanes)
        weighted[span, :] = (jac[span, :].astype(jnp.float32) * scale).astype(jnp.bfloat16)


def pick_kernel(unit, info, *refs):
    pieces, out, position = refs[:-2], refs[-2], refs[-1]
    listed, _, tile = out.shape
    block = lax.axis_index("obs")
    units = pieces[0].shape[1] // unit
    for a in range(position.shape[0]):
        position[a] = -1
    for k in range(listed):
        position[info[k]] = k
    for step, piece in enumerate(pieces):
        for u in range(units):
            row = ((block ^ step) * units + u) * unit
            at = position[row // tile]
            for q in range(tile // unit):

                @pl.when((at >= 0) & (row % tile == q * unit))
                def _():
                    out[at, :, q * unit:(q + 1) * unit] = piece[:, u * unit:(u + 1) * unit]


def product_kernel(held, weighted, *refs):
    pieces, outs, probe = refs[:len(refs) // 2], refs[len(refs) // 2:-1], refs[-1]
    listed, high, tile = pieces[0].shape
    for j, piece in enumerate(pieces):
        for k in range(listed):
            probe[j * high:(j + 1) * high, k * tile:(k + 1) * tile] = piece[k]
    image = lax.dot_general(probe[...], held[...], CONTRACT_LAST, preferred_element_type=jnp.float32)
    image = image.astype(jnp.bfloat16)
    for n in range(0, held.shape[1], COLUMNS):
        product = jnp.dot(image, weighted[:, n:n + COLUMNS], preferred_element_type=jnp.float32)
        for j, out in enumerate(outs):
            out[:, n:n + COLUMNS] = product[j * high:(j + 1) * high, :].astype(out.dtype)


def place_kernel(unit, tile, listed, parts_count, info, *refs):
    parts, outs = refs[:parts_count], refs[parts_count:-2]
    position, total = refs[-2:]
    block = lax.axis_index("obs")
    for a in range(position.shape[0]):
        position[a] = -1
    for k in range(listed):
        position[info[listed + info[k]]] = k
    value = parts[0][...]
    for term in parts[1:]:
        value = value + term[...].astype(jnp.float32)
    total[...] = value
    units = outs[0].shape[1] // unit
    for step, out in enumerate(outs):
        for u in range(units):
            row = ((block ^ step) * units + u) * unit
            at = position[row // tile]
            first = pl.multiple_of(jnp.maximum(at, 0) * tile, tile)
            whole = jnp.where(at >= 0, total[:, pl.ds(first, tile)], 0.0)
            taken = whole[:, :unit]
            for q in range(1, tile // unit):
                taken = jnp.where(row % tile == q * unit, whole[:, q * unit:(q + 1) * unit], taken)
            out[:, u * unit:(u + 1) * unit] = taken.astype(out.dtype)


def kept(step, direct):
    return jnp.float32 if step == 0 or step >= direct and step % 2 == 0 else jnp.bfloat16


def local(obs_count, subs, jacobian, obs_weight, row_counts, tile_lists, tile_slot, probe_block):
    rows, width = jacobian.shape
    tiles = tile_slot.shape[0]
    listed = tile_lists.shape[1]
    tile = width // listed
    own_rows, probe_width = probe_block.shape
    unit = min(own_rows, tile)
    high = probe_width // subs
    my_list = lax.dynamic_index_in_dim(tile_lists, lax.axis_index("obs"), 0, keepdims=False)
    info = jnp.concatenate([my_list, tile_slot])

    def params(mib):
        return pltpu.CompilerParams(vmem_limit_bytes=mib * MIB)

    share = pl.pallas_call(
        share_kernel,
        out_shape=jax.ShapeDtypeStruct((high, own_rows), jnp.bfloat16),
        in_specs=[VMEM],
        out_specs=VMEM,
        compiler_params=params(8),
        name="share_probe",
    )(probe_block)
    pick = pl.pallas_call(
        functools.partial(pick_kernel, unit),
        out_shape=jax.ShapeDtypeStruct((listed, high, tile), jnp.bfloat16),
        in_specs=[SMEM] + [VMEM] * obs_count,
        out_specs=VMEM,
        scratch_shapes=[pltpu.SMEM((tiles,), jnp.int32)],
        compiler_params=params(8),
        name="pick_listed",
    )
    weight_lanes = min(128, rows)
    observation = lax.axis_index("sub") * rows + jnp.arange(rows, dtype=jnp.int32)
    weight = obs_weight * (observation < row_counts[0]).astype(jnp.float32)
    weight = weight.reshape(rows // weight_lanes, weight_lanes)
    info, weight = lax.optimization_barrier((info, weight))
    picked = pick(info, *spread(share, "obs", obs_count, SPREAD_DIRECT))
    weighted = pl.pallas_call(
        weigh_kernel,
        out_shape=jax.ShapeDtypeStruct((rows, width), jnp.bfloat16),
        in_specs=[VMEM, VMEM, pl.BlockSpec(memory_space=pl.ANY)],
        out_specs=VMEM,
        compiler_params=params(16),
        cost_estimate=pl.CostEstimate(flops=2 * rows * width, bytes_accessed=4 * rows * width, transcendentals=0),
        name="weigh",
    )(weight, jacobian, picked)

    product = pl.pallas_call(
        product_kernel,
        out_shape=[jax.ShapeDtypeStruct((high, width), kept(j, SUB_DIRECT)) for j in range(subs)],
        in_specs=[VMEM] * (2 + subs),
        out_specs=[VMEM] * subs,
        scratch_shapes=[pltpu.VMEM((probe_width, width), jnp.bfloat16)],
        compiler_params=params(24),
        cost_estimate=pl.CostEstimate(
            flops=4 * rows * width * probe_width, bytes_accessed=4 * rows * width, transcendentals=0),
        name="product",
    )
    place = pl.pallas_call(
        functools.partial(place_kernel, unit, tile, listed, subs // 2 + 1),
        out_shape=[jax.ShapeDtypeStruct((high, own_rows), kept(step, OBS_DIRECT)) for step in range(obs_count)],
        in_specs=[SMEM] + [VMEM] * (subs // 2 + 1),
        out_specs=[VMEM] * obs_count,
        scratch_shapes=[pltpu.SMEM((tiles,), jnp.int32), pltpu.VMEM((high, width), jnp.float32)],
        compiler_params=params(8),
        name="place",
    )

    columns = spread(picked, "sub", subs, SPREAD_DIRECT, (weighted,))
    first, later = collect(product(jacobian, weighted, *columns), "sub", subs, SUB_DIRECT)
    first, later = collect(place(info, *first, *later), "obs", obs_count, OBS_DIRECT)
    total = after(sum(term.astype(jnp.float32) for term in first))
    return sum((term.astype(jnp.float32) for term in later), total).T.astype(jnp.bfloat16)


def solution(mesh):
    placed = (P(("obs", "sub"), None), P(("obs", "sub")), P("obs"), P(), P(), P("obs", None))
    return jax.shard_map(
        functools.partial(local, mesh.shape["obs"], mesh.shape["sub"]),
        mesh=mesh, in_specs=placed, out_specs=P("obs", "sub"), check_vma=False,
    )
```

```python
import functools

import jax
import jax.numpy as jnp
from jax import lax
from jax.experimental import pallas as pl
from jax.experimental.pallas import tpu as pltpu
from jax.sharding import PartitionSpec as P

MIB = 1024 * 1024
SPREAD_DIRECT = 2
SUB_DIRECT = 2
OBS_DIRECT = 4
COLUMNS = 512
CONTRACT_LAST = (((1,), (1,)), ((), ()))
SMEM = pl.BlockSpec(memory_space=pltpu.SMEM)
VMEM = pl.BlockSpec(memory_space=pltpu.VMEM)
HBM = pl.BlockSpec(memory_space=pltpu.HBM)


def swap(value, axis, count, step):
    return lax.ppermute(value, axis, [(i, i ^ step) for i in range(count)])


def after(value, *before):
    return lax.optimization_barrier((value, *before))[0]


def spread(value, axis, count, direct, before=()):
    held = {0: value}
    far = range(count - 2, direct - 1, -2)
    for step in (*far, *range(min(direct, count) - 1, 0, -1)):
        held[step] = swap(value, axis, count, step)
    for step in far:
        held[step + 1] = swap(after(held[step], *before), axis, count, 1)
    return [held[step] for step in range(count)]


def collect_far(terms, axis, count, direct):
    parts, ready = [], ()
    for step in range(count - 2, direct - 1, -2):
        passed = swap(terms[step + 1], axis, count, 1)
        ready = (terms[step] + passed.astype(jnp.float32)).astype(jnp.bfloat16),
        parts.append(swap(*ready, axis, count, step))
    return parts, ready


def collect_near(terms, axis, count, direct, ready):
    first, later = [terms[0], swap(terms[1], axis, count, 1)], []
    for step in range(min(direct, count) - 1, 1, -1):
        if step % 2:
            later.append(swap(after(terms[step], *ready), axis, count, step))
        else:
            first.append(swap(terms[step], axis, count, step))
    return first, later


def share_kernel(probe, out):
    high, width = out.shape[0], probe.shape[1]
    first = lax.axis_index("sub") * high
    row = lax.broadcasted_iota(jnp.int32, (high, width), 0)
    column = lax.broadcasted_iota(jnp.int32, (high, width), 1)
    wanted = (column == row + first).astype(jnp.bfloat16)
    out[...] = lax.dot_general(wanted, probe[...], CONTRACT_LAST, preferred_element_type=jnp.float32).astype(out.dtype)


def weigh_kernel(weight, jac, after, weighted):
    rows, width = jac.shape
    lanes = weight.shape[1]
    for i in range(rows // lanes):
        scale = jnp.broadcast_to(weight[i:i + 1, :], (lanes, lanes)).T
        scale = jnp.concatenate([scale] * (width // lanes), axis=1)
        span = slice(i * lanes, (i + 1) * lanes)
        weighted[span, :] = (jac[span, :].astype(jnp.float32) * scale).astype(jnp.bfloat16)


def pick_kernel(unit, info, *refs):
    pieces, out, position = refs[:-2], refs[-2], refs[-1]
    listed, _, tile = out.shape
    block = lax.axis_index("obs")
    units = pieces[0].shape[1] // unit
    for a in range(position.shape[0]):
        position[a] = -1
    for k in range(listed):
        position[info[k]] = k
    for step, piece in enumerate(pieces):
        for u in range(units):
            row = ((block ^ step) * units + u) * unit
            at = position[row // tile]
            for q in range(tile // unit):

                @pl.when((at >= 0) & (row % tile == q * unit))
                def _():
                    out[at, :, q * unit:(q + 1) * unit] = piece[:, u * unit:(u + 1) * unit]


def product_kernel(held, weighted, *refs):
    pieces, outs, probe = refs[:len(refs) // 2], refs[len(refs) // 2:-1], refs[-1]
    listed, high, tile = pieces[0].shape
    for j, piece in enumerate(pieces):
        for k in range(listed):
            probe[j * high:(j + 1) * high, k * tile:(k + 1) * tile] = piece[k]
    image = lax.dot_general(probe[...], held[...], CONTRACT_LAST, preferred_element_type=jnp.float32)
    image = image.astype(jnp.bfloat16)
    for n in range(0, held.shape[1], COLUMNS):
        product = jnp.dot(image, weighted[:, n:n + COLUMNS], preferred_element_type=jnp.float32)
        for j, out in enumerate(outs):
            out[:, n:n + COLUMNS] = product[j * high:(j + 1) * high, :].astype(out.dtype)


def place_kernel(unit, tile, listed, parts_count, info, *refs):
    parts, outs = refs[:parts_count], refs[parts_count:-2]
    position, total = refs[-2:]
    block = lax.axis_index("obs")
    for a in range(position.shape[0]):
        position[a] = -1
    for k in range(listed):
        position[info[listed + info[k]]] = k
    value = parts[0][...]
    for term in parts[1:]:
        value = value + term[...].astype(jnp.float32)
    total[...] = value
    units = outs[0].shape[1] // unit
    for step, out in enumerate(outs):
        for u in range(units):
            row = ((block ^ step) * units + u) * unit
            at = position[row // tile]
            first = pl.multiple_of(jnp.maximum(at, 0) * tile, tile)
            whole = jnp.where(at >= 0, total[:, pl.ds(first, tile)], 0.0)
            taken = whole[:, :unit]
            for q in range(1, tile // unit):
                taken = jnp.where(row % tile == q * unit, whole[:, q * unit:(q + 1) * unit], taken)
            out[:, u * unit:(u + 1) * unit] = taken.astype(out.dtype)


def kept(step, direct):
    return jnp.float32 if step == 0 or step >= direct and step % 2 == 0 else jnp.bfloat16


def local(obs_count, subs, jacobian, obs_weight, row_counts, tile_lists, tile_slot, probe_block):
    rows, width = jacobian.shape
    tiles = tile_slot.shape[0]
    listed = tile_lists.shape[1]
    tile = width // listed
    own_rows, probe_width = probe_block.shape
    unit = min(own_rows, tile)
    high = probe_width // subs
    my_list = lax.dynamic_index_in_dim(tile_lists, lax.axis_index("obs"), 0, keepdims=False)
    info = jnp.concatenate([my_list, tile_slot])

    def params(mib):
        return pltpu.CompilerParams(vmem_limit_bytes=mib * MIB)

    share = pl.pallas_call(
        share_kernel,
        out_shape=jax.ShapeDtypeStruct((high, own_rows), jnp.bfloat16),
        in_specs=[VMEM],
        out_specs=VMEM,
        compiler_params=params(8),
        name="share_probe",
    )(probe_block)
    pick = pl.pallas_call(
        functools.partial(pick_kernel, unit),
        out_shape=jax.ShapeDtypeStruct((listed, high, tile), jnp.bfloat16),
        in_specs=[SMEM] + [VMEM] * obs_count,
        out_specs=VMEM,
        scratch_shapes=[pltpu.SMEM((tiles,), jnp.int32)],
        compiler_params=params(8),
        name="pick_listed",
    )
    weight_lanes = min(128, rows)
    observation = lax.axis_index("sub") * rows + jnp.arange(rows, dtype=jnp.int32)
    weight = obs_weight * (observation < row_counts[0]).astype(jnp.float32)
    weight = weight.reshape(rows // weight_lanes, weight_lanes)
    info, weight = lax.optimization_barrier((info, weight))
    picked = pick(info, *spread(share, "obs", obs_count, SPREAD_DIRECT))
    weighted = pl.pallas_call(
        weigh_kernel,
        out_shape=jax.ShapeDtypeStruct((rows, width), jnp.bfloat16),
        in_specs=[VMEM, VMEM, pl.BlockSpec(memory_space=pl.ANY)],
        out_specs=VMEM,
        compiler_params=params(16),
        cost_estimate=pl.CostEstimate(flops=2 * rows * width, bytes_accessed=4 * rows * width, transcendentals=0),
        name="weigh",
    )(weight, jacobian, picked)

    def product(name, steps, columns):
        lanes = high * len(steps)
        return pl.pallas_call(
            product_kernel,
            out_shape=[jax.ShapeDtypeStruct((high, width), kept(j, SUB_DIRECT)) for j in steps],
            in_specs=[VMEM] * (2 + len(steps)),
            out_specs=[VMEM] * len(steps),
            scratch_shapes=[pltpu.VMEM((lanes, width), jnp.bfloat16)],
            compiler_params=params(24),
            cost_estimate=pl.CostEstimate(
                flops=4 * rows * width * lanes, bytes_accessed=4 * rows * width, transcendentals=0),
            name=name,
        )(jacobian, weighted, *columns)

    place = pl.pallas_call(
        functools.partial(place_kernel, unit, tile, listed, 2),
        out_shape=[jax.ShapeDtypeStruct((high, own_rows), kept(step, OBS_DIRECT)) for step in range(obs_count)],
        in_specs=[SMEM] + [VMEM] * 2,
        out_specs=[VMEM] * obs_count,
        scratch_shapes=[pltpu.SMEM((tiles,), jnp.int32), pltpu.VMEM((high, width), jnp.float32)],
        compiler_params=params(8),
        name="place",
    )

    columns = spread(picked, "sub", subs, SPREAD_DIRECT, (weighted,))
    terms = {}
    if subs > 2:
        terms = dict(enumerate(product("far_product", range(2, subs), columns[2:]), 2))
    far, ready = collect_far(terms, "sub", subs, SUB_DIRECT)
    near = product("near_product", range(2), [columns[0], after(columns[1], *ready)])
    first, _ = collect_near(near, "sub", subs, SUB_DIRECT, ready)
    partial = sum((term.astype(jnp.float32) for term in far), first[0])
    terms = place(info, partial, first[1])
    far, ready = collect_far(terms, "obs", obs_count, OBS_DIRECT)
    first, later = collect_near(terms, "obs", obs_count, OBS_DIRECT, ready)
    first += far
    total = after(sum(term.astype(jnp.float32) for term in first))
    return sum((term.astype(jnp.float32) for term in later), total).T.astype(jnp.bfloat16)


def solution(mesh):
    placed = (P(("obs", "sub"), None), P(("obs", "sub")), P("obs"), P(), P(), P("obs", None))
    return jax.shard_map(
        functools.partial(local, mesh.shape["obs"], mesh.shape["sub"]),
        mesh=mesh, in_specs=placed, out_specs=P("obs", "sub"), check_vma=False,
    )
```

```python
import functools

import jax
import jax.numpy as jnp
from jax import lax
from jax.experimental import pallas as pl
from jax.experimental.pallas import tpu as pltpu
from jax.sharding import PartitionSpec as P

MIB = 1024 * 1024
SPREAD_DIRECT = 2
SUB_DIRECT = 2
OBS_DIRECT = 4
COLUMNS = 512
CONTRACT_LAST = (((1,), (1,)), ((), ()))
SMEM = pl.BlockSpec(memory_space=pltpu.SMEM)
VMEM = pl.BlockSpec(memory_space=pltpu.VMEM)
HBM = pl.BlockSpec(memory_space=pltpu.HBM)


def swap(value, axis, count, step):
    return lax.ppermute(value, axis, [(i, i ^ step) for i in range(count)])


def after(value, *before):
    return lax.optimization_barrier((value, *before))[0]


def spread(value, axis, count, direct, before=()):
    held = {0: value}
    far = range(count - 2, direct - 1, -2)
    for step in (*far, *range(min(direct, count) - 1, 0, -1)):
        held[step] = swap(value, axis, count, step)
    for step in far:
        held[step + 1] = swap(after(held[step], *before), axis, count, 1)
    return [held[step] for step in range(count)]


def collect_far(terms, axis, count, direct):
    parts, ready = [], ()
    for step in range(count - 2, direct - 1, -2):
        passed = swap(terms[step + 1], axis, count, 1)
        ready = (terms[step] + passed.astype(jnp.float32)).astype(jnp.bfloat16),
        parts.append(swap(*ready, axis, count, step))
    return parts, ready


def collect_near(terms, axis, count, direct, ready):
    first, later = [terms[0], swap(terms[1], axis, count, 1)], []
    for step in range(min(direct, count) - 1, 1, -1):
        if step % 2:
            later.append(swap(after(terms[step], *ready), axis, count, step))
        else:
            first.append(swap(terms[step], axis, count, step))
    return first, later


def share_kernel(probe, out):
    high, width = out.shape[0], probe.shape[1]
    first = lax.axis_index("sub") * high
    row = lax.broadcasted_iota(jnp.int32, (high, width), 0)
    column = lax.broadcasted_iota(jnp.int32, (high, width), 1)
    wanted = (column == row + first).astype(jnp.bfloat16)
    out[...] = lax.dot_general(wanted, probe[...], CONTRACT_LAST, preferred_element_type=jnp.float32).astype(out.dtype)


def weigh_kernel(weight, jac, after, weighted):
    rows, width = jac.shape
    lanes = weight.shape[1]
    for i in range(rows // lanes):
        scale = jnp.broadcast_to(weight[i:i + 1, :], (lanes, lanes)).T
        scale = jnp.concatenate([scale] * (width // lanes), axis=1)
        span = slice(i * lanes, (i + 1) * lanes)
        weighted[span, :] = (jac[span, :].astype(jnp.float32) * scale).astype(jnp.bfloat16)


def pick_kernel(unit, info, *refs):
    pieces, out, position = refs[:-2], refs[-2], refs[-1]
    listed, _, tile = out.shape
    block = lax.axis_index("obs")
    units = pieces[0].shape[1] // unit
    for a in range(position.shape[0]):
        position[a] = -1
    for k in range(listed):
        position[info[k]] = k
    for step, piece in enumerate(pieces):
        for u in range(units):
            row = ((block ^ step) * units + u) * unit
            at = position[row // tile]
            for q in range(tile // unit):

                @pl.when((at >= 0) & (row % tile == q * unit))
                def _():
                    out[at, :, q * unit:(q + 1) * unit] = piece[:, u * unit:(u + 1) * unit]


def product_kernel(held, weighted, *refs):
    pieces, outs, probe = refs[:len(refs) // 2], refs[len(refs) // 2:-1], refs[-1]
    listed, high, tile = pieces[0].shape
    for j, piece in enumerate(pieces):
        for k in range(listed):
            probe[j * high:(j + 1) * high, k * tile:(k + 1) * tile] = piece[k]
    image = lax.dot_general(probe[...], held[...], CONTRACT_LAST, preferred_element_type=jnp.float32)
    image = image.astype(jnp.bfloat16)
    for n in range(0, held.shape[1], COLUMNS):
        product = jnp.dot(image, weighted[:, n:n + COLUMNS], preferred_element_type=jnp.float32)
        for j, out in enumerate(outs):
            out[:, n:n + COLUMNS] = product[j * high:(j + 1) * high, :].astype(out.dtype)


def merge_kernel(term, passed, held, weighted, own, beside, both, first, second, probe):
    both[...] = (term[...] + passed[...].astype(jnp.float32)).astype(both.dtype)

    @pl.when(lax.axis_index("sub") % 2 == 1)
    def _():
        product_kernel(held, weighted, own, beside, first, second, probe)


def near_kernel(_, __, held, weighted, own, beside, first, second, probe):
    @pl.when(lax.axis_index("sub") % 2 == 0)
    def _():
        product_kernel(held, weighted, own, beside, first, second, probe)


def place_kernel(unit, tile, listed, parts_count, info, *refs):
    parts, outs = refs[:parts_count], refs[parts_count:-2]
    position, total = refs[-2:]
    block = lax.axis_index("obs")
    for a in range(position.shape[0]):
        position[a] = -1
    for k in range(listed):
        position[info[listed + info[k]]] = k
    value = parts[0][...]
    for term in parts[1:]:
        value = value + term[...].astype(jnp.float32)
    total[...] = value
    units = outs[0].shape[1] // unit
    for step, out in enumerate(outs):
        for u in range(units):
            row = ((block ^ step) * units + u) * unit
            at = position[row // tile]
            first = pl.multiple_of(jnp.maximum(at, 0) * tile, tile)
            whole = jnp.where(at >= 0, total[:, pl.ds(first, tile)], 0.0)
            taken = whole[:, :unit]
            for q in range(1, tile // unit):
                taken = jnp.where(row % tile == q * unit, whole[:, q * unit:(q + 1) * unit], taken)
            out[:, u * unit:(u + 1) * unit] = taken.astype(out.dtype)


def kept(step, direct):
    return jnp.float32 if step == 0 or step >= direct and step % 2 == 0 else jnp.bfloat16


def local(obs_count, subs, jacobian, obs_weight, row_counts, tile_lists, tile_slot, probe_block):
    rows, width = jacobian.shape
    tiles = tile_slot.shape[0]
    listed = tile_lists.shape[1]
    tile = width // listed
    own_rows, probe_width = probe_block.shape
    unit = min(own_rows, tile)
    high = probe_width // subs
    my_list = lax.dynamic_index_in_dim(tile_lists, lax.axis_index("obs"), 0, keepdims=False)
    info = jnp.concatenate([my_list, tile_slot])

    def params(mib):
        return pltpu.CompilerParams(vmem_limit_bytes=mib * MIB)

    share = pl.pallas_call(
        share_kernel,
        out_shape=jax.ShapeDtypeStruct((high, own_rows), jnp.bfloat16),
        in_specs=[VMEM],
        out_specs=VMEM,
        compiler_params=params(8),
        name="share_probe",
    )(probe_block)
    pick = pl.pallas_call(
        functools.partial(pick_kernel, unit),
        out_shape=jax.ShapeDtypeStruct((listed, high, tile), jnp.bfloat16),
        in_specs=[SMEM] + [VMEM] * obs_count,
        out_specs=VMEM,
        scratch_shapes=[pltpu.SMEM((tiles,), jnp.int32)],
        compiler_params=params(8),
        name="pick_listed",
    )
    weight_lanes = min(128, rows)
    observation = lax.axis_index("sub") * rows + jnp.arange(rows, dtype=jnp.int32)
    weight = obs_weight * (observation < row_counts[0]).astype(jnp.float32)
    weight = weight.reshape(rows // weight_lanes, weight_lanes)
    info, weight = lax.optimization_barrier((info, weight))
    picked = pick(info, *spread(share, "obs", obs_count, SPREAD_DIRECT))
    weighted = pl.pallas_call(
        weigh_kernel,
        out_shape=jax.ShapeDtypeStruct((rows, width), jnp.bfloat16),
        in_specs=[VMEM, VMEM, pl.BlockSpec(memory_space=pl.ANY)],
        out_specs=VMEM,
        compiler_params=params(16),
        cost_estimate=pl.CostEstimate(flops=2 * rows * width, bytes_accessed=4 * rows * width, transcendentals=0),
        name="weigh",
    )(weight, jacobian, picked)

    def product(name, steps, columns):
        lanes = high * len(steps)
        return pl.pallas_call(
            product_kernel,
            out_shape=[jax.ShapeDtypeStruct((high, width), kept(j, SUB_DIRECT)) for j in steps],
            in_specs=[VMEM] * (2 + len(steps)),
            out_specs=[VMEM] * len(steps),
            scratch_shapes=[pltpu.VMEM((lanes, width), jnp.bfloat16)],
            compiler_params=params(24),
            cost_estimate=pl.CostEstimate(
                flops=4 * rows * width * lanes, bytes_accessed=4 * rows * width, transcendentals=0),
            name=name,
        )(jacobian, weighted, *columns)

    place = pl.pallas_call(
        functools.partial(place_kernel, unit, tile, listed, 2),
        out_shape=[jax.ShapeDtypeStruct((high, own_rows), kept(step, OBS_DIRECT)) for step in range(obs_count)],
        in_specs=[SMEM] + [VMEM] * 2,
        out_specs=[VMEM] * obs_count,
        scratch_shapes=[pltpu.SMEM((tiles,), jnp.int32), pltpu.VMEM((high, width), jnp.float32)],
        compiler_params=params(8),
        name="place",
    )

    columns = spread(picked, "sub", subs, SPREAD_DIRECT, (weighted,))
    terms = dict(enumerate(product("far_product", range(2, subs), columns[2:]), 2))
    far = []
    for step in range(subs - 2, 2, -2):
        passed = swap(terms[step + 1], "sub", subs, 1)
        both = (terms[step] + passed.astype(jnp.float32)).astype(jnp.bfloat16)
        far.append(swap(both, "sub", subs, step))
    near_shapes = [jax.ShapeDtypeStruct((high, width), kept(j, SUB_DIRECT)) for j in range(2)]
    near_probe = [pltpu.VMEM((2 * high, width), jnp.bfloat16)]
    near_cost = pl.CostEstimate(flops=8 * rows * width * high, bytes_accessed=4 * rows * width, transcendentals=0)
    both, *near = pl.pallas_call(
        merge_kernel,
        out_shape=[jax.ShapeDtypeStruct((high, width), jnp.bfloat16)] + near_shapes,
        in_specs=[VMEM] * 6,
        out_specs=[VMEM] * 3,
        scratch_shapes=near_probe,
        compiler_params=params(24),
        name="merge",
    )(terms[2], swap(terms[3], "sub", subs, 1), jacobian, weighted, *columns[:2])
    far.append(swap(both, "sub", subs, 2))
    near = pl.pallas_call(
        near_kernel,
        out_shape=near_shapes,
        in_specs=[VMEM] * 6,
        out_specs=[VMEM] * 2,
        scratch_shapes=near_probe,
        input_output_aliases={0: 0, 1: 1},
        compiler_params=params(24),
        cost_estimate=near_cost,
        name="near_product",
    )(*near, jacobian, weighted, *columns[:2])
    first, _ = collect_near(near, "sub", subs, SUB_DIRECT, ())
    partial = sum((term.astype(jnp.float32) for term in far), first[0])
    terms = place(info, partial, first[1])
    far, ready = collect_far(terms, "obs", obs_count, OBS_DIRECT)
    first, later = collect_near(terms, "obs", obs_count, OBS_DIRECT, ready)
    first += far
    total = after(sum(term.astype(jnp.float32) for term in first))
    return sum((term.astype(jnp.float32) for term in later), total).T.astype(jnp.bfloat16)


def solution(mesh):
    placed = (P(("obs", "sub"), None), P(("obs", "sub")), P("obs"), P(), P(), P("obs", None))
    return jax.shard_map(
        functools.partial(local, mesh.shape["obs"], mesh.shape["sub"]),
        mesh=mesh, in_specs=placed, out_specs=P("obs", "sub"), check_vma=False,
    )
```

```python
import functools

import jax
import jax.numpy as jnp
from jax import lax
from jax.experimental import pallas as pl
from jax.experimental.pallas import tpu as pltpu
from jax.sharding import PartitionSpec as P

MIB = 1024 * 1024
SPREAD_DIRECT = 2
SUB_DIRECT = 2
OBS_DIRECT = 4
COLUMNS = 512
CONTRACT_LAST = (((1,), (1,)), ((), ()))
SMEM = pl.BlockSpec(memory_space=pltpu.SMEM)
VMEM = pl.BlockSpec(memory_space=pltpu.VMEM)
HBM = pl.BlockSpec(memory_space=pltpu.HBM)


def swap(value, axis, count, step):
    return lax.ppermute(value, axis, [(i, i ^ step) for i in range(count)])


def after(value, *before):
    return lax.optimization_barrier((value, *before))[0]


def spread(value, axis, count, direct, before=()):
    held = {0: value}
    far = range(count - 2, direct - 1, -2)
    for step in (*far, *range(min(direct, count) - 1, 0, -1)):
        held[step] = swap(value, axis, count, step)
    for step in far:
        held[step + 1] = swap(after(held[step], *before), axis, count, 1)
    return [held[step] for step in range(count)]


def collect_far(terms, axis, count, direct):
    parts, ready = [], ()
    for step in range(count - 2, direct - 1, -2):
        passed = swap(terms[step + 1], axis, count, 1)
        ready = (terms[step] + passed.astype(jnp.float32)).astype(jnp.bfloat16),
        parts.append(swap(*ready, axis, count, step))
    return parts, ready


def collect_near(terms, axis, count, direct, ready):
    first, later = [terms[0], swap(terms[1], axis, count, 1)], []
    for step in range(min(direct, count) - 1, 1, -1):
        if step % 2:
            later.append(swap(after(terms[step], *ready), axis, count, step))
        else:
            first.append(swap(terms[step], axis, count, step))
    return first, later


def share_kernel(probe, out):
    high, width = out.shape[0], probe.shape[1]
    first = lax.axis_index("sub") * high
    row = lax.broadcasted_iota(jnp.int32, (high, width), 0)
    column = lax.broadcasted_iota(jnp.int32, (high, width), 1)
    wanted = (column == row + first).astype(jnp.bfloat16)
    out[...] = lax.dot_general(wanted, probe[...], CONTRACT_LAST, preferred_element_type=jnp.float32).astype(out.dtype)


def weigh_kernel(weight, jac, after, weighted):
    rows, width = jac.shape
    lanes = weight.shape[1]
    for i in range(rows // lanes):
        scale = jnp.broadcast_to(weight[i:i + 1, :], (lanes, lanes)).T
        scale = jnp.concatenate([scale] * (width // lanes), axis=1)
        span = slice(i * lanes, (i + 1) * lanes)
        weighted[span, :] = (jac[span, :].astype(jnp.float32) * scale).astype(jnp.bfloat16)


def pick_kernel(unit, steps, info, *refs):
    pieces, out, position = refs[-2 - len(steps):-2], refs[-2], refs[-1]
    listed, _, tile = out.shape
    block = lax.axis_index("obs")
    units = pieces[0].shape[1] // unit
    for a in range(position.shape[0]):
        position[a] = -1
    for k in range(listed):
        position[info[k]] = k
    for step, piece in zip(steps, pieces):
        for u in range(units):
            row = ((block ^ step) * units + u) * unit
            at = position[row // tile]
            for q in range(tile // unit):

                @pl.when((at >= 0) & (row % tile == q * unit))
                def _():
                    out[at, :, q * unit:(q + 1) * unit] = piece[:, u * unit:(u + 1) * unit]


def product_kernel(held, weighted, *refs):
    pieces, outs, probe = refs[:len(refs) // 2], refs[len(refs) // 2:-1], refs[-1]
    listed, high, tile = pieces[0].shape
    for j, piece in enumerate(pieces):
        for k in range(listed):
            probe[j * high:(j + 1) * high, k * tile:(k + 1) * tile] = piece[k]
    image = lax.dot_general(probe[...], held[...], CONTRACT_LAST, preferred_element_type=jnp.float32)
    image = image.astype(jnp.bfloat16)
    for n in range(0, held.shape[1], COLUMNS):
        product = jnp.dot(image, weighted[:, n:n + COLUMNS], preferred_element_type=jnp.float32)
        for j, out in enumerate(outs):
            out[:, n:n + COLUMNS] = product[j * high:(j + 1) * high, :].astype(out.dtype)


def place_kernel(unit, tile, listed, parts_count, info, *refs):
    parts, outs = refs[:parts_count], refs[parts_count:-2]
    position, total = refs[-2:]
    block = lax.axis_index("obs")
    for a in range(position.shape[0]):
        position[a] = -1
    for k in range(listed):
        position[info[listed + info[k]]] = k
    value = parts[0][...]
    for term in parts[1:]:
        value = value + term[...].astype(jnp.float32)
    total[...] = value
    units = outs[0].shape[1] // unit
    for step, out in enumerate(outs):
        for u in range(units):
            row = ((block ^ step) * units + u) * unit
            at = position[row // tile]
            first = pl.multiple_of(jnp.maximum(at, 0) * tile, tile)
            whole = jnp.where(at >= 0, total[:, pl.ds(first, tile)], 0.0)
            taken = whole[:, :unit]
            for q in range(1, tile // unit):
                taken = jnp.where(row % tile == q * unit, whole[:, q * unit:(q + 1) * unit], taken)
            out[:, u * unit:(u + 1) * unit] = taken.astype(out.dtype)


def kept(step, direct):
    return jnp.float32 if step == 0 or step >= direct and step % 2 == 0 else jnp.bfloat16


def local(obs_count, subs, jacobian, obs_weight, row_counts, tile_lists, tile_slot, probe_block):
    rows, width = jacobian.shape
    tiles = tile_slot.shape[0]
    listed = tile_lists.shape[1]
    tile = width // listed
    own_rows, probe_width = probe_block.shape
    unit = min(own_rows, tile)
    high = probe_width // subs
    my_list = lax.dynamic_index_in_dim(tile_lists, lax.axis_index("obs"), 0, keepdims=False)
    info = jnp.concatenate([my_list, tile_slot])

    def params(mib):
        return pltpu.CompilerParams(vmem_limit_bytes=mib * MIB)

    share = pl.pallas_call(
        share_kernel,
        out_shape=jax.ShapeDtypeStruct((high, own_rows), jnp.bfloat16),
        in_specs=[VMEM],
        out_specs=VMEM,
        compiler_params=params(8),
        name="share_probe",
    )(probe_block)
    def pick(name, steps, info, *before):
        held = [pieces[step] for step in steps]
        return pl.pallas_call(
            functools.partial(pick_kernel, unit, steps),
            out_shape=jax.ShapeDtypeStruct((listed, high, tile), jnp.bfloat16),
            in_specs=[SMEM] + [VMEM] * (len(before) + len(held)),
            out_specs=VMEM,
            scratch_shapes=[pltpu.SMEM((tiles,), jnp.int32)],
            input_output_aliases={1: 0} if before else {},
            compiler_params=params(8),
            name=name,
        )(info, *before, *held)

    weight_lanes = min(128, rows)
    observation = lax.axis_index("sub") * rows + jnp.arange(rows, dtype=jnp.int32)
    weight = obs_weight * (observation < row_counts[0]).astype(jnp.float32)
    weight = weight.reshape(rows // weight_lanes, weight_lanes)
    pieces = spread(share, "obs", obs_count, SPREAD_DIRECT)
    last = obs_count // 2 + 1
    picked = pick("pick_listed", [step for step in range(obs_count) if step != last], info)
    info, weight = lax.optimization_barrier((info, weight))
    picked = pick("pick_last", [last], info, picked)
    weighted = pl.pallas_call(
        weigh_kernel,
        out_shape=jax.ShapeDtypeStruct((rows, width), jnp.bfloat16),
        in_specs=[VMEM, VMEM, pl.BlockSpec(memory_space=pl.ANY)],
        out_specs=VMEM,
        compiler_params=params(16),
        cost_estimate=pl.CostEstimate(flops=2 * rows * width, bytes_accessed=4 * rows * width, transcendentals=0),
        name="weigh",
    )(weight, jacobian, picked)

    def product(name, steps, columns):
        lanes = high * len(steps)
        return pl.pallas_call(
            product_kernel,
            out_shape=[jax.ShapeDtypeStruct((high, width), kept(j, SUB_DIRECT)) for j in steps],
            in_specs=[VMEM] * (2 + len(steps)),
            out_specs=[VMEM] * len(steps),
            scratch_shapes=[pltpu.VMEM((lanes, width), jnp.bfloat16)],
            compiler_params=params(24),
            cost_estimate=pl.CostEstimate(
                flops=4 * rows * width * lanes, bytes_accessed=4 * rows * width, transcendentals=0),
            name=name,
        )(jacobian, weighted, *columns)

    place = pl.pallas_call(
        functools.partial(place_kernel, unit, tile, listed, 2),
        out_shape=[jax.ShapeDtypeStruct((high, own_rows), kept(step, OBS_DIRECT)) for step in range(obs_count)],
        in_specs=[SMEM] + [VMEM] * 2,
        out_specs=[VMEM] * obs_count,
        scratch_shapes=[pltpu.SMEM((tiles,), jnp.int32), pltpu.VMEM((high, width), jnp.float32)],
        compiler_params=params(8),
        name="place",
    )

    columns = spread(picked, "sub", subs, SPREAD_DIRECT, (weighted,))
    terms = {}
    if subs > 2:
        terms = dict(enumerate(product("far_product", range(2, subs), columns[2:]), 2))
    far, ready = collect_far(terms, "sub", subs, SUB_DIRECT)
    near = product("near_product", range(2), [columns[0], after(columns[1], *ready)])
    first, _ = collect_near(near, "sub", subs, SUB_DIRECT, ready)
    partial = sum((term.astype(jnp.float32) for term in far), first[0])
    terms = place(info, partial, first[1])
    far, ready = collect_far(terms, "obs", obs_count, OBS_DIRECT)
    first, later = collect_near(terms, "obs", obs_count, OBS_DIRECT, ready)
    first += far
    total = after(sum(term.astype(jnp.float32) for term in first))
    return sum((term.astype(jnp.float32) for term in later), total).T.astype(jnp.bfloat16)


def solution(mesh):
    placed = (P(("obs", "sub"), None), P(("obs", "sub")), P("obs"), P(), P(), P("obs", None))
    return jax.shard_map(
        functools.partial(local, mesh.shape["obs"], mesh.shape["sub"]),
        mesh=mesh, in_specs=placed, out_specs=P("obs", "sub"), check_vma=False,
    )
```
